32 devices in a mesh: batch: 4 (over y, x), ctx: 8 (over z, core).
Axes of the slice: x: 2, y: 2, z: 4, core: 2. Of those that a mesh axis runs over, the one named last changes fastest.
Arguments:
- tokens: bfloat16 [4096, 768], P(('batch', 'ctx')), may hold values from -12 to 12
- lengths: int32 [4], P('batch'), may hold values from 897 to 1024
- w_query: bfloat16 [768, 768], P(('batch', 'ctx')), may hold values from -0.21875 to 0.21875
- b_query: bfloat16 [768], P(('batch', 'ctx')), may hold values from -3 to 3
- w_key: bfloat16 [768, 768], P(('batch', 'ctx')), may hold values from -0.21875 to 0.21875
- w_value: bfloat16 [768, 768], P(('batch', 'ctx')), may hold values from -0.21875 to 0.21875
- b_value: bfloat16 [768], P(('batch', 'ctx')), may hold values from -0.1875 to 0.1875
- w_out: bfloat16 [768, 768], P(('batch', 'ctx')), may hold values from -7 to 7
- b_out: bfloat16 [768], P(('batch', 'ctx')), may hold values from -3 to 3
- gain_one: bfloat16 [768], P(('batch', 'ctx')), may hold values from 0.5 to 1.5
- shift_one: bfloat16 [768], P(('batch', 'ctx')), may hold values from -1.75 to 1.75
- w_up: bfloat16 [768, 3072], P(('batch', 'ctx')), may hold values from -0.21875 to 0.21875
- b_up: bfloat16 [3072], P(('batch', 'ctx')), may hold values from -3 to 3
- w_down: bfloat16 [3072, 768], P(('batch', 'ctx')), may hold values from -0.15625 to 0.15625
- b_down: bfloat16 [768], P(('batch', 'ctx')), may hold values from -1.75 to 1.75
- gain_two: bfloat16 [768], P(('batch', 'ctx')), may hold values from 0.5 to 1.5
- shift_two: bfloat16 [768], P(('batch', 'ctx')), may hold values from -3 to 3
- cotangent: bfloat16 [4096, 768], P(('batch', 'ctx')), may hold values from -6 to 6
Outputs:
- output: bfloat16 [4096, 768], P(('batch', 'ctx'))
- grad_tokens: bfloat16 [4096, 768], P(('batch', 'ctx'))
- grad_w_query: float32 [768, 768], P(('batch', 'ctx'))
- grad_b_query: float32 [768], P(('batch', 'ctx'))
- grad_w_key: float32 [768, 768], P(('batch', 'ctx'))
- grad_w_value: float32 [768, 768], P(('batch', 'ctx'))
- grad_b_value: float32 [768], P(('batch', 'ctx'))
- grad_w_out: float32 [768, 768], P(('batch', 'ctx'))
- grad_b_out: float32 [768], P(('batch', 'ctx'))
- grad_gain_one: float32 [768], P(('batch', 'ctx'))
- grad_shift_one: float32 [768], P(('batch', 'ctx'))
- grad_w_up: float32 [768, 3072], P(('batch', 'ctx'))
- grad_b_up: float32 [3072], P(('batch', 'ctx'))
- grad_w_down: float32 [3072, 768], P(('batch', 'ctx'))
- grad_b_down: float32 [768], P(('batch', 'ctx'))
- grad_gain_two: float32 [768], P(('batch', 'ctx'))
- grad_shift_two: float32 [768], P(('batch', 'ctx'))
The draws below stay inside these ranges and needn't reach their ends.
Inputs may be any that keep to these rules, and one draw needn't show every extreme that they name: `lengths`: valid positions of each sequence; positions from this length on are padding.
All inputs are finite; a program needn't handle non-finite values.
Results may differ from the reference program's by a relative error of at most 0.025.
Values may be sent and summed in bfloat16 or wider, within the bound.
No kernel may reach another device: no remote copies, remote signals or barrier semaphores. Data moves between devices by JAX's collectives and lax.ppermute only.
A program may use at most 128 MiB of HBM per device.

```python
import math
import jax
import jax.numpy as jnp
from jax import lax

D = 768
HEADS = 12
HEAD_DIM = 64
FF = 3072
TOK_DEV = 128
LENGTH = 1024
SEQS = 4
TOKENS = 4096


def touch_ends(drawn, own_key, smallest, top_value):
    spot = [jax.random.randint(jax.random.fold_in(own_key, axis), (), 0, length) for axis, length in enumerate(drawn.shape)]
    longest = drawn.shape.index(max(drawn.shape))
    neighbour = spot[:longest] + [(spot[longest] + 1) % drawn.shape[longest]] + spot[longest + 1:]
    return drawn.at[tuple(spot)].set(smallest).at[tuple(neighbour)].set(top_value)


def spiked(values, rng, source, target, parts, factor):
    owner, partner = [(jnp.arange(values.shape[axis_at]) // (values.shape[axis_at] // parts)).reshape([-1 if axis == axis_at else 1 for axis in range(values.ndim)]) for axis_at in (source, target)]
    chosen = jax.random.permutation(rng, parts)[partner]
    strong = (owner == chosen) | (owner == (partner + parts // 2) % parts)
    return jnp.where(strong, factor * values, values)


def shard_levels(stream_key, dims, cuts, low, top_value):
    level, own = 1.0, jax.random.fold_in(stream_key, 6)
    for axis_at, blocks in cuts:
        draws = jnp.exp(jax.random.uniform(jax.random.fold_in(own, axis_at), (blocks,), jnp.float32, low / len(cuts), top_value / len(cuts)))
        level = level * jnp.repeat(draws, dims[axis_at] // blocks).reshape([-1 if axis == axis_at else 1 for axis in range(len(dims))])
    return level


def centred(own_key, shape, scale, limit, split=(), kind=jnp.bfloat16):
    drawn = scale * jax.random.normal(own_key, shape, jnp.float32)
    if split:
        drawn = drawn * shard_levels(own_key, shape, split, -0.22, 0.18)
    return jnp.clip(drawn, -limit, limit).astype(kind)


def gaussian_with(key, extent, scale, bound, pieces, heavy, kind=jnp.bfloat16):
    entries = scale * jax.random.normal(key, extent, jnp.float32)
    if pieces:
        entries = entries * shard_levels(key, extent, pieces, -0.22, 0.18)
    return jnp.clip(spiked(entries, jax.random.fold_in(key, 3), *heavy), -bound, bound).astype(kind)


def setup_inputs(seed: int = 0) -> dict:
    arg_keys = jax.random.split(jax.random.key(seed), 19)
    return {
        "tokens": gaussian_with(arg_keys[0], (TOKENS, D), 1.0, 12.0, ((0, 32),), (0, 1, 32, 2.75)),
        "lengths": touch_ends(jax.random.randint(arg_keys[1], (SEQS,), LENGTH - TOK_DEV + 1, LENGTH + 1), jax.random.fold_in(arg_keys[1], 1), LENGTH - TOK_DEV + 1, LENGTH).astype(jnp.int32),
        "w_query": centred(arg_keys[2], (D, D), D ** -0.5, 0.21875, ((0, 32),)),
        "b_query": centred(arg_keys[3], (D,), 0.5, 3.0, ((0, 32),)),
        "w_key": centred(arg_keys[4], (D, D), D ** -0.5, 0.21875, ((0, 32),)),
        "w_value": centred(arg_keys[5], (D, D), D ** -0.5, 0.21875, ((0, 32),)),
        "b_value": centred(arg_keys[6], (D,), (LENGTH ** -0.5), 0.1875, ((0, 32),)),
        "w_out": centred(arg_keys[7], (D, D), ((LENGTH ** 0.5) * (D ** -0.5)), 7.0, ((0, 32),)),
        "b_out": centred(arg_keys[8], (D,), 0.5, 3.0, ((0, 32),)),
        "gain_one": jnp.clip(1.0 + 0.1 * jax.random.normal(arg_keys[9], (D,), jnp.float32), 0.5, 1.5).astype(jnp.bfloat16),
        "shift_one": centred(arg_keys[10], (D,), 0.3, 1.75, ((0, 32),)),
        "w_up": centred(arg_keys[11], (D, FF), D ** -0.5, 0.21875, ((0, 32),)),
        "b_up": centred(arg_keys[12], (FF,), 0.5, 3.0, ((0, 32),)),
        "w_down": centred(arg_keys[13], (FF, D), (FF // 2) ** -0.5, 0.15625, ((0, 32),)),
        "b_down": centred(arg_keys[14], (D,), 0.3, 1.75, ((0, 32),)),
        "gain_two": jnp.clip(1.0 + 0.1 * jax.random.normal(arg_keys[15], (D,), jnp.float32), 0.5, 1.5).astype(jnp.bfloat16),
        "shift_two": centred(arg_keys[16], (D,), 0.5, 3.0, ((0, 32),)),
        "cotangent": centred(arg_keys[17], (TOKENS, D), 1.0, 6.0, ((0, 32),)),
    }


@jax.custom_vjp
def low(v):
    return lax.optimization_barrier(v.astype(jnp.bfloat16)).astype(jnp.float32)

@jax.custom_vjp
def low_back(v):
    return v

def low_keep(v):
    return (low(v), None)

def low_pass(kept, grad):
    return (grad,)

def back_keep(v):
    return (v, None)

def back_low(kept, grad):
    return (low(grad),)
low.defvjp(low_keep, low_pass)
low_back.defvjp(back_keep, back_low)
highest = lax.Precision.HIGHEST
epsilon = 1e-06
masked_score = -1e+30

def matmul(left, right):
    return jnp.dot(left, right, precision=highest)

def normalize(resid, gain, shift):
    center = resid - lax.optimization_barrier(jnp.mean(resid, -1, keepdims=True))
    spread = lax.optimization_barrier(jnp.mean(center * center, -1, keepdims=True))
    return center * lax.rsqrt(spread + epsilon) * gain + shift

def attend_block(query_block, seq_keys, seq_values, valid):
    raw = jnp.einsum('qhd,khd->hqk', query_block, seq_keys, precision=highest) * HEAD_DIM ** (-0.5)
    scores = jnp.where(valid[None, None, :], low_back(raw), masked_score)
    top = lax.optimization_barrier(jnp.max(scores, axis=-1, keepdims=True))
    expos = jnp.exp(scores - top)
    total = lax.optimization_barrier(jnp.sum(expos, axis=-1))
    weights = low(expos)
    summed = jnp.einsum('hqk,khd->qhd', weights, seq_values, precision=highest)
    return summed / jnp.transpose(total)[:, :, None]

def attention(query, keys, values, lengths):
    block = math.gcd(LENGTH, 512)
    count = LENGTH // block
    query_blocks = query.reshape(SEQS, count, block, HEADS, HEAD_DIM)
    key_heads = keys.reshape(SEQS, LENGTH, HEADS, HEAD_DIM)
    value_heads = values.reshape(SEQS, LENGTH, HEADS, HEAD_DIM)

    def per_sequence(items):
        seq_query, seq_keys, seq_values, seq_length = items
        valid = jnp.arange(LENGTH, dtype=jnp.int32) < seq_length

        def one_block(query_block):
            return attend_block(query_block, seq_keys, seq_values, valid)
        return lax.map(jax.checkpoint(one_block), seq_query)
    attended = lax.map(per_sequence, (query_blocks, key_heads, value_heads, lengths))
    return attended.reshape(TOKENS, D)

def layer_forward(tokens, w_query, b_query, w_key, w_value, b_value, w_out, b_out, gain_one, shift_one, w_up, b_up, w_down, b_down, gain_two, shift_two, lengths):
    query = low(low_back(matmul(tokens, w_query) + b_query))
    keys = low(low_back(matmul(tokens, w_key)))
    values = low(low_back(matmul(tokens, w_value) + b_value))
    attended = attention(query, keys, values, lengths)
    mixed = low(low_back(attended))
    projected = low_back(matmul(mixed, w_out) + b_out)
    first = normalize(tokens + projected, gain_one, shift_one)
    first_low = low(first)
    inner = low_back(matmul(first_low, w_up) + b_up)
    active = low(jax.nn.gelu(inner, approximate=False))
    branch = low_back(matmul(active, w_down) + b_down)
    return normalize(first + branch, gain_two, shift_two)

def reference(tokens, lengths, w_query, b_query, w_key, w_value, b_value, w_out, b_out, gain_one, shift_one, w_up, b_up, w_down, b_down, gain_two, shift_two, cotangent):
    floats = [item.astype(jnp.float32) for item in (tokens, w_query, b_query, w_key, w_value, b_value, w_out, b_out, gain_one, shift_one, w_up, b_up, w_down, b_down, gain_two, shift_two)]

    def forward(*params):
        return layer_forward(*params, lengths)
    result, pullback = jax.vjp(forward, *floats)
    grads = pullback(cotangent.astype(jnp.float32))
    return (result.astype(jnp.bfloat16), grads[0].astype(jnp.bfloat16), grads[1], grads[2], grads[3], grads[4], grads[5], grads[6], grads[7], grads[8], grads[9], grads[10], grads[11], grads[12], grads[13], grads[14], grads[15])
```

```python
import functools
import math

import jax
import jax.numpy as jnp
from jax import lax
from jax.experimental import pallas as pl
from jax.experimental.pallas import tpu as pltpu
from jax.sharding import PartitionSpec as P

HEADS = 12
HEAD_DIM = 64


epsilon = 1e-06
masked_score = -1e30


def shifted(block, axis, distance):
    devices = range(lax.axis_size(axis))
    route = [((i - distance) % len(devices), i) for i in devices]
    return lax.ppermute(block, axis, route)


def normalize(resid, gain, shift):
    center = resid - jnp.mean(resid, -1, keepdims=True)
    spread = jnp.mean(center * center, -1, keepdims=True)
    return center * lax.rsqrt(spread + epsilon) * gain + shift


def gelu_exact(value):
    return jax.nn.gelu(value, approximate=False)


def head_scores(query_blk, key_blk, owner, length):
    count = key_blk.shape[0]
    raw = jnp.einsum(
        "qhd,khd->hqk",
        query_blk.reshape(-1, HEADS, HEAD_DIM),
        key_blk.reshape(count, HEADS, HEAD_DIM),
        preferred_element_type=jnp.float32,
    )
    position = owner * count + jnp.arange(count, dtype=jnp.int32)
    return jnp.where((position < length)[None, None, :], raw * HEAD_DIM ** (-0.5), masked_score)


def block_grads(query_blk, grad_blk, log_blk, delta_blk, key_blk, value_blk, owner, length):
    rows = query_blk.shape[0]
    count = key_blk.shape[0]
    scores = head_scores(query_blk, key_blk, owner, length)
    probs = jnp.exp(scores - log_blk[:, :, None])
    probs_low = probs.astype(jnp.bfloat16)
    grad_heads = grad_blk.reshape(rows, HEADS, HEAD_DIM)
    query_heads = query_blk.reshape(rows, HEADS, HEAD_DIM)
    key_heads = key_blk.reshape(count, HEADS, HEAD_DIM)
    value_heads = value_blk.reshape(count, HEADS, HEAD_DIM)
    prob_grad = jnp.einsum(
        "qhd,khd->hqk", grad_heads, value_heads, preferred_element_type=jnp.float32
    )
    score_grad = (probs * (prob_grad - delta_blk[:, :, None])).astype(jnp.bfloat16)
    value_term = jnp.einsum(
        "hqk,qhd->khd", probs_low, grad_heads, preferred_element_type=jnp.float32
    )
    key_term = jnp.einsum(
        "hqk,qhd->khd", score_grad, query_heads, preferred_element_type=jnp.float32
    ) * HEAD_DIM ** (-0.5)
    query_term = jnp.einsum(
        "hqk,khd->qhd", score_grad, key_heads, preferred_element_type=jnp.float32
    ) * HEAD_DIM ** (-0.5)
    return (
        query_term.reshape(rows, -1),
        key_term.reshape(count, -1),
        value_term.reshape(count, -1),
    )


def body(
    tokens,
    lengths,
    w_query,
    b_query,
    w_key,
    w_value,
    b_value,
    w_out,
    b_out,
    gain_one,
    shift_one,
    w_up,
    b_up,
    w_down,
    b_down,
    gain_two,
    shift_two,
    cotangent,
):
    cycle = lax.axis_size("ctx")
    place = lax.axis_index("ctx")
    length = lengths[0]
    rows = tokens.shape[0]
    width = tokens.shape[1]
    gathered = (
        lax.all_gather(w_query, ("batch", "ctx"), axis=0, tiled=True),
        lax.all_gather(w_key, ("batch", "ctx"), axis=0, tiled=True),
        lax.all_gather(w_value, ("batch", "ctx"), axis=0, tiled=True),
        lax.all_gather(w_out, ("batch", "ctx"), axis=0, tiled=True),
        lax.all_gather(w_up, ("batch", "ctx"), axis=0, tiled=True),
        lax.all_gather(w_down, ("batch", "ctx"), axis=0, tiled=True),
        lax.all_gather(b_query, ("batch", "ctx"), axis=0, tiled=True),
        lax.all_gather(b_value, ("batch", "ctx"), axis=0, tiled=True),
        lax.all_gather(b_out, ("batch", "ctx"), axis=0, tiled=True),
        lax.all_gather(gain_one, ("batch", "ctx"), axis=0, tiled=True),
        lax.all_gather(shift_one, ("batch", "ctx"), axis=0, tiled=True),
        lax.all_gather(b_up, ("batch", "ctx"), axis=0, tiled=True),
        lax.all_gather(b_down, ("batch", "ctx"), axis=0, tiled=True),
        lax.all_gather(gain_two, ("batch", "ctx"), axis=0, tiled=True),
        lax.all_gather(shift_two, ("batch", "ctx"), axis=0, tiled=True),
    )
    query_full, key_full, value_full, out_full, up_full, down_full = gathered[:6]
    small = [item.astype(jnp.float32) for item in gathered[6:]]
    (
        bias_query,
        bias_value,
        bias_out,
        gain_first,
        shift_first,
        bias_up,
        bias_down,
        gain_second,
        shift_second,
    ) = small
    query_low = (
        jnp.dot(tokens, query_full, preferred_element_type=jnp.float32) + bias_query
    ).astype(jnp.bfloat16)
    key_low = jnp.dot(tokens, key_full, preferred_element_type=jnp.float32).astype(jnp.bfloat16)
    value_low = (
        jnp.dot(tokens, value_full, preferred_element_type=jnp.float32) + bias_value
    ).astype(jnp.bfloat16)
    start_top = jnp.full((HEADS, rows), masked_score, jnp.float32)
    start_total = jnp.zeros((HEADS, rows), jnp.float32)
    start_sum = jnp.zeros((rows, HEADS, HEAD_DIM), jnp.float32)

    def running(state, pair, owner):
        top, total, summed = state
        scores = head_scores(query_low, pair[0], owner, length)
        new_top = jnp.maximum(top, jnp.max(scores, -1))
        factor = jnp.exp(top - new_top)
        expos = jnp.exp(scores - new_top[:, :, None])
        total = total * factor + jnp.sum(expos, -1)
        summed = summed * factor.T[:, :, None] + jnp.einsum(
            "hqk,khd->qhd",
            expos.astype(jnp.bfloat16),
            pair[1].reshape(-1, HEADS, HEAD_DIM),
            preferred_element_type=jnp.float32,
        )
        return (new_top, total, summed)

    def run_step(step, carry):
        pair, state = carry
        state = running(state, pair, (place - step) % cycle)
        pair = shifted((pair[0], pair[1]), "ctx", 1)
        return (pair, state)

    pair, state = lax.fori_loop(
        0, cycle - 1, run_step, ((key_low, value_low), (start_top, start_total, start_sum))
    )
    top, total, summed = running(state, pair, (place + 1) % cycle)
    log_total = top + jnp.log(total)
    attended = (summed / total.T[:, :, None]).reshape(rows, width)
    mixed = attended.astype(jnp.bfloat16)
    projected = jnp.dot(mixed, out_full, preferred_element_type=jnp.float32) + bias_out
    first, first_back = jax.vjp(
        normalize, tokens.astype(jnp.float32) + projected, gain_first, shift_first
    )
    first_low = first.astype(jnp.bfloat16)
    inner = jnp.dot(first_low, up_full, preferred_element_type=jnp.float32) + bias_up
    active, gelu_back = jax.vjp(gelu_exact, inner)
    active_low = active.astype(jnp.bfloat16)
    branch = jnp.dot(active_low, down_full, preferred_element_type=jnp.float32) + bias_down
    result, second_back = jax.vjp(normalize, first + branch, gain_second, shift_second)
    output = result.astype(jnp.bfloat16)
    query_back, key_back, value_back, out_back, up_back, down_back = (
        query_full,
        key_full,
        value_full,
        out_full,
        up_full,
        down_full,
    )
    grad_second, grad_gain_two, grad_shift_two = second_back(cotangent.astype(jnp.float32))
    branch_grad = grad_second.astype(jnp.bfloat16)
    grad_b_down = jnp.sum(branch_grad.astype(jnp.float32), 0)
    grad_w_down = jnp.einsum(
        "tf,td->fd", active_low, branch_grad, preferred_element_type=jnp.float32
    )
    active_grad = jnp.einsum(
        "td,fd->tf", branch_grad, down_back, preferred_element_type=jnp.float32
    )
    inner_grad = gelu_back(active_grad)[0].astype(jnp.bfloat16)
    grad_b_up = jnp.sum(inner_grad.astype(jnp.float32), 0)
    grad_w_up = jnp.einsum("td,tf->df", first_low, inner_grad, preferred_element_type=jnp.float32)
    first_grad = (
        jnp.einsum("tf,df->td", inner_grad, up_back, preferred_element_type=jnp.float32)
        + grad_second
    )
    grad_first, grad_gain_one, grad_shift_one = first_back(first_grad)
    proj_grad = grad_first.astype(jnp.bfloat16)
    grad_b_out = jnp.sum(proj_grad.astype(jnp.float32), 0)
    grad_w_out = jnp.einsum("td,te->de", mixed, proj_grad, preferred_element_type=jnp.float32)
    mixed_grad = jnp.einsum(
        "te,de->td", proj_grad, out_back, preferred_element_type=jnp.float32
    ).astype(jnp.bfloat16)
    delta = jnp.sum(
        (mixed_grad.astype(jnp.float32) * attended).reshape(rows, HEADS, HEAD_DIM), -1
    ).T
    zeros = jnp.zeros((rows, width), jnp.float32)

    def move_key_grads(grads):
        return (
            shifted(grads[0].astype(jnp.bfloat16), "ctx", 1).astype(jnp.float32),
            shifted(grads[1].astype(jnp.bfloat16), "ctx", 1).astype(jnp.float32),
        )

    def key_step(step, carry):
        blocks, grads, query_acc = carry
        query_term, key_term, value_term = block_grads(
            query_low,
            mixed_grad,
            log_total,
            delta,
            blocks[0],
            blocks[1],
            (place - step) % cycle,
            length,
        )
        grads = move_key_grads((grads[0] + key_term, grads[1] + value_term))
        blocks = shifted((blocks[0], blocks[1]), "ctx", 1)
        return (blocks, grads, query_acc + query_term)

    blocks, grads, query_acc = lax.fori_loop(
        0, cycle - 1, key_step, ((key_low, value_low), (zeros, zeros), zeros)
    )
    query_term, key_term, value_term = block_grads(
        query_low, mixed_grad, log_total, delta, blocks[0], blocks[1], (place + 1) % cycle, length
    )
    key_acc, value_acc = move_key_grads((grads[0] + key_term, grads[1] + value_term))
    query_acc = query_acc + query_term
    query_grad = query_acc.astype(jnp.bfloat16)
    key_grad = key_acc.astype(jnp.bfloat16)
    value_grad = value_acc.astype(jnp.bfloat16)
    grad_b_query = jnp.sum(query_grad.astype(jnp.float32), 0)
    grad_b_value = jnp.sum(value_grad.astype(jnp.float32), 0)
    grad_w_query = jnp.einsum("td,te->de", tokens, query_grad, preferred_element_type=jnp.float32)
    grad_w_key = jnp.einsum("td,te->de", tokens, key_grad, preferred_element_type=jnp.float32)
    grad_w_value = jnp.einsum("td,te->de", tokens, value_grad, preferred_element_type=jnp.float32)
    token_grad = grad_first + jnp.einsum(
        "te,de->td", query_grad, query_back, preferred_element_type=jnp.float32
    )
    token_grad = token_grad + jnp.einsum(
        "te,de->td", key_grad, key_back, preferred_element_type=jnp.float32
    )
    token_grad = token_grad + jnp.einsum(
        "te,de->td", value_grad, value_back, preferred_element_type=jnp.float32
    )
    grad_tokens = token_grad.astype(jnp.bfloat16)
    sharded = (
        lax.psum_scatter(grad_w_query, ("batch", "ctx"), scatter_dimension=0, tiled=True),
        lax.psum_scatter(grad_b_query, ("batch", "ctx"), scatter_dimension=0, tiled=True),
        lax.psum_scatter(grad_w_key, ("batch", "ctx"), scatter_dimension=0, tiled=True),
        lax.psum_scatter(grad_w_value, ("batch", "ctx"), scatter_dimension=0, tiled=True),
        lax.psum_scatter(grad_b_value, ("batch", "ctx"), scatter_dimension=0, tiled=True),
        lax.psum_scatter(grad_w_out, ("batch", "ctx"), scatter_dimension=0, tiled=True),
        lax.psum_scatter(grad_b_out, ("batch", "ctx"), scatter_dimension=0, tiled=True),
        lax.psum_scatter(grad_gain_one, ("batch", "ctx"), scatter_dimension=0, tiled=True),
        lax.psum_scatter(grad_shift_one, ("batch", "ctx"), scatter_dimension=0, tiled=True),
        lax.psum_scatter(grad_w_up, ("batch", "ctx"), scatter_dimension=0, tiled=True),
        lax.psum_scatter(grad_b_up, ("batch", "ctx"), scatter_dimension=0, tiled=True),
        lax.psum_scatter(grad_w_down, ("batch", "ctx"), scatter_dimension=0, tiled=True),
        lax.psum_scatter(grad_b_down, ("batch", "ctx"), scatter_dimension=0, tiled=True),
        lax.psum_scatter(grad_gain_two, ("batch", "ctx"), scatter_dimension=0, tiled=True),
        lax.psum_scatter(grad_shift_two, ("batch", "ctx"), scatter_dimension=0, tiled=True),
    )
    return (
        output,
        grad_tokens,
        sharded[0],
        sharded[1],
        sharded[2],
        sharded[3],
        sharded[4],
        sharded[5],
        sharded[6],
        sharded[7],
        sharded[8],
        sharded[9],
        sharded[10],
        sharded[11],
        sharded[12],
        sharded[13],
        sharded[14],
    )


def normal_parts(resid):
    center = resid - jnp.mean(resid, -1, keepdims=True)
    spread = jnp.mean(center * center, -1, keepdims=True)
    scale = lax.rsqrt(spread + epsilon)
    return center * scale, scale


def normal_back(hat, scale, grad):
    inner = jnp.mean(grad * hat, -1, keepdims=True)
    return scale * (grad - jnp.mean(grad, -1, keepdims=True) - hat * inner)


def dot(left, right, dims=((1,), (0,))):
    return lax.dot_general(left, right, (dims, ((), ())), preferred_element_type=jnp.float32)


def head_rows(block, head, extra):
    row = lax.broadcasted_iota(jnp.int32, block.shape, 0)
    keep = (row >= head * HEAD_DIM) & (row < (head + 1) * HEAD_DIM)
    if extra:
        keep = keep | (row >= extra)
    return jnp.where(keep, block, jnp.zeros_like(block))


def head_lanes(block, head):
    lane = lax.broadcasted_iota(jnp.int32, block.shape, 1)
    keep = (lane >= head * HEAD_DIM) & (lane < (head + 1) * HEAD_DIM)
    return jnp.where(keep, block, jnp.zeros_like(block))


def attend_kernel(heads, query_t, key, value_t, att_ref, mixed_ref, log_ref):
    width = heads * HEAD_DIM
    pieces = mixed_ref.shape[0]
    span = mixed_ref.shape[2]
    logs = []
    for head in range(heads):
        scores = dot(key[...], head_rows(query_t[...], head, width))
        top = jnp.max(scores, 0, keepdims=True)
        expos = jnp.exp(scores - top)
        total = jnp.sum(expos, 0, keepdims=True)
        rows = slice(head * HEAD_DIM, (head + 1) * HEAD_DIM)
        summed = dot(value_t[rows, :], expos.astype(jnp.bfloat16)) / total
        att_ref[rows, :] = summed
        low = summed.astype(jnp.bfloat16)
        for piece in range(pieces):
            mixed_ref[piece, rows, :] = low[:, piece * span : (piece + 1) * span]
        logs.append(top + jnp.log(total))
    for head in range(heads):
        log_ref[head : head + 1, :] = logs[head]


def attend_back_kernel(
    heads,
    query_t,
    query,
    key,
    key_t,
    value,
    grad_t,
    grad,
    att,
    log,
    query_grad,
    key_grad,
    value_grad,
):
    width = heads * HEAD_DIM

    @pl.when(pl.program_id(0) == 0)
    def _():
        key_grad[...] = jnp.zeros_like(key_grad)
        value_grad[...] = jnp.zeros_like(value_grad)

    turned = []
    for head in range(heads):
        rows = slice(head * HEAD_DIM, (head + 1) * HEAD_DIM)
        scores = dot(key[...], head_rows(query_t[...], head, width))
        probs = jnp.exp(scores - log[head : head + 1, :])
        prob_grad = dot(value[...], head_rows(grad_t[...], head, 0))
        delta = jnp.sum(grad_t[rows, :].astype(jnp.float32) * att[rows, :], 0, keepdims=True)
        score_grad = (probs * (prob_grad - delta)).astype(jnp.bfloat16)
        turned.append(dot(key_t[rows, :], score_grad))
        key_grad[...] += dot(score_grad, head_lanes(query[...], head))
        value_grad[...] += dot(probs.astype(jnp.bfloat16), head_lanes(grad[...], head))
    gathered = jnp.concatenate(turned, 0) * HEAD_DIM ** (-0.5)
    query_grad[...] = jnp.transpose(gathered).astype(jnp.bfloat16)


def attend(heads, query_t, key, value_t, span):
    count = query_t.shape[1]
    keys = key.shape[0]
    width = heads * HEAD_DIM
    pieces = 2 if (count // span) % 2 == 0 else 1
    step = pieces * span
    return pl.pallas_call(
        functools.partial(attend_kernel, heads),
        grid=(count // step,),
        in_specs=[
            pl.BlockSpec((query_t.shape[0], step), lambda i: (0, i)),
            pl.BlockSpec(key.shape, lambda i: (0, 0)),
            pl.BlockSpec(value_t.shape, lambda i: (0, 0)),
        ],
        out_specs=[
            pl.BlockSpec((width, step), lambda i: (0, i)),
            pl.BlockSpec((pieces, width, span), lambda i: (i, 0, 0)),
            pl.BlockSpec((heads, step), lambda i: (0, i)),
        ],
        out_shape=[
            jax.ShapeDtypeStruct((width, count), jnp.float32),
            jax.ShapeDtypeStruct((count // span, width, span), jnp.bfloat16),
            jax.ShapeDtypeStruct((heads, count), jnp.float32),
        ],
        compiler_params=pltpu.CompilerParams(vmem_limit_bytes=40 * 2**20),
        cost_estimate=pl.CostEstimate(
            flops=4 * heads * count * keys * 256,
            bytes_accessed=4 * keys * 256 * 2,
            transcendentals=heads * count * keys,
        ),
        name="attend",
    )(query_t, key, value_t)


def attend_back(heads, span, query_t, query, key, key_t, value, grad_t, grad, att, log):
    count = query_t.shape[1]
    keys = key.shape[0]
    width = heads * HEAD_DIM
    pieces = 2 if (count // span) % 2 == 0 else 1
    step = pieces * span

    def lanes(block):
        return pl.BlockSpec((block.shape[0], step), lambda i: (0, i))

    def rows(block):
        return pl.BlockSpec((step, block.shape[1]), lambda i: (i, 0))

    def whole(block):
        return pl.BlockSpec(block.shape, lambda i: (0, 0))

    return pl.pallas_call(
        functools.partial(attend_back_kernel, heads),
        grid=(count // step,),
        in_specs=[
            lanes(query_t),
            rows(query),
            whole(key),
            whole(key_t),
            whole(value),
            lanes(grad_t),
            rows(grad),
            lanes(att),
            lanes(log),
        ],
        out_specs=[
            pl.BlockSpec((step, width), lambda i: (i, 0)),
            pl.BlockSpec((keys, width), lambda i: (0, 0)),
            pl.BlockSpec((keys, width), lambda i: (0, 0)),
        ],
        out_shape=[
            jax.ShapeDtypeStruct((count, width), jnp.bfloat16),
            jax.ShapeDtypeStruct((keys, width), jnp.float32),
            jax.ShapeDtypeStruct((keys, width), jnp.float32),
        ],
        compiler_params=pltpu.CompilerParams(vmem_limit_bytes=40 * 2**20),
        cost_estimate=pl.CostEstimate(
            flops=10 * heads * count * keys * 256,
            bytes_accessed=8 * keys * 256 * 2,
            transcendentals=heads * count * keys,
        ),
        name="attend_back",
    )(query_t, query, key, key_t, value, grad_t, grad, att, log)


def pick(blocks, index, axis=0):
    return lax.dynamic_index_in_dim(blocks, index, axis, keepdims=False)


def ordered(found, me):
    count = len(found)
    rising = [found[count - 1 - i] for i in range(count)]
    twice = jnp.stack(rising + rising[:-1], 0)
    return lax.dynamic_slice_in_dim(twice, count - 1 - me, count, 0)


def layer_split(
    tokens,
    lengths,
    w_query,
    b_query,
    w_key,
    w_value,
    b_value,
    w_out,
    b_out,
    gain_one,
    shift_one,
    w_up,
    b_up,
    w_down,
    b_down,
    gain_two,
    shift_two,
    cotangent,
):
    f32, low = jnp.float32, jnp.bfloat16
    teams = lax.axis_size("batch")
    chips = lax.axis_size("ctx") // 2
    team = lax.axis_index("batch")
    place = lax.axis_index("ctx")
    chip, core = place // 2, place % 2
    rows, width = tokens.shape
    part = w_query.shape[0]
    hidden = w_up.shape[1]
    quarter = hidden // teams
    heads = HEADS // chips
    group = heads * HEAD_DIM
    length = lengths[0]

    def to_chip(block, distance):
        route = [(i, (i // 2 + distance) % chips * 2 + i % 2) for i in range(2 * chips)]
        return lax.ppermute(block, "ctx", route)

    def to_core(block):
        return lax.ppermute(block, "ctx", [(i, i ^ 1) for i in range(2 * chips)])

    def to_team(block, distance):
        return lax.ppermute(block, "batch", [(i, (i + distance) % teams) for i in range(teams)])

    def from_chips(block):
        return [block] + [to_chip(block, d) for d in range(1, chips)]

    def from_teams(block):
        return [block] + [to_team(block, d) for d in range(1, teams)]

    def swap_chips(blocks, axis=0):
        return [pick(blocks, chip, axis)] + [
            to_chip(pick(blocks, (chip + d) % chips, axis), d) for d in range(1, chips)
        ]

    def swap_teams(blocks, axis=0):
        return [pick(blocks, team, axis)] + [
            to_team(pick(blocks, (team + d) % teams, axis), d) for d in range(1, teams)
        ]

    def both_cores(block, axis):
        other = to_core(block)
        first = jnp.where(core == 0, block, other)
        second = jnp.where(core == 0, other, block)
        return jnp.stack([first, second], axis)

    def total(blocks):
        result = blocks[0].astype(f32)
        for block in blocks[1:]:
            result = result + block.astype(f32)
        return result

    def return_teams(blocks):
        return total(
            [blocks[0]] + [to_team(blocks[d].astype(low), -d) for d in range(1, teams)]
        )

    vectors = (
        b_query,
        b_value,
        b_out,
        gain_one,
        shift_one,
        b_down,
        gain_two,
        shift_two,
        b_up,
    )
    short = jnp.concatenate(vectors)
    held = -(-(part + 1) // 16) * 16
    by_group = jnp.concatenate(
        [item.reshape(part, chips, group) for item in (w_query, w_key, w_value)], 2
    ).transpose(1, 0, 2)
    short_row = jnp.pad(short, (0, 3 * group - short.shape[0]))
    packed = jnp.concatenate(
        [
            by_group,
            jnp.broadcast_to(short_row, (chips, 1, 3 * group)),
            jnp.zeros((chips, held - part - 1, 3 * group), low),
        ],
        1,
    )
    mine_rel = from_chips(tokens)
    packed = ordered(swap_chips(packed), chip)
    packed = ordered(from_teams(packed), team)
    packed = both_cores(packed, 2)
    w_heads = packed[:, :, :, :part].reshape(width, 3 * group)
    shorts = packed[:, :, :, part].reshape(teams * chips * 2, 3 * group)

    def vector(index, size):
        return shorts[:, index * part : index * part + size].reshape(-1).astype(f32)

    bias_query, bias_value, bias_out, gain_first, shift_first = [vector(i, part) for i in range(5)]
    bias_down, gain_second, shift_second = [vector(i, part) for i in range(5, 8)]
    bias_up = vector(8, b_up.shape[0])
    bias_up = lax.dynamic_slice_in_dim(bias_up, team * quarter, quarter)
    bias_query = lax.dynamic_slice_in_dim(bias_query, chip * group, group)
    bias_value = lax.dynamic_slice_in_dim(bias_value, chip * group, group)

    other_rel = [to_core(block) for block in mine_rel]
    mine = jnp.concatenate(mine_rel, 0)
    every = jnp.concatenate(mine_rel + other_rel, 0)
    starts = [((chip - d) % chips * 2 + core) * rows for d in range(chips)]
    starts = starts + [((chip - d) % chips * 2 + 1 - core) * rows for d in range(chips)]
    position = jnp.concatenate([start + jnp.arange(rows) for start in starts])

    up_blocks = ordered(swap_teams(w_up.reshape(part, teams, quarter), 1), team)
    up_blocks = ordered(from_chips(up_blocks), chip)
    up_blocks = both_cores(up_blocks, 2)
    up_part = up_blocks.transpose(1, 0, 2, 3, 4).reshape(width, quarter)
    down_blocks = ordered(from_chips(w_down), chip)
    down_part = both_cores(down_blocks, 1).reshape(quarter, width)
    out_blocks = ordered(from_chips(w_out), chip)
    out_blocks = ordered(from_teams(out_blocks), team)
    out_full = both_cores(out_blocks, 2).reshape(width, width)

    w_q, w_k, w_v = w_heads[:, :group], w_heads[:, group : 2 * group], w_heads[:, 2 * group :]
    scale = HEAD_DIM ** (-0.5)
    nt, tn = ((0,), (1,)), ((0,), (0,))
    query = ((dot(mine, w_q) + bias_query).astype(low) * scale).astype(low)
    query_t = ((dot(w_q, mine, nt) + bias_query[:, None]).astype(low) * scale).astype(low)
    key = dot(every, w_k).astype(low)
    key_t = dot(w_k, every, nt).astype(low)
    value = (dot(every, w_v) + bias_value).astype(low)
    value_t = (dot(w_v, every, nt) + bias_value[:, None]).astype(low)
    hide = jnp.where(position < length, 0.0, masked_score).astype(low)
    spare = 256 - group % 256
    key_wide = jnp.concatenate(
        [key, hide[:, None], jnp.zeros((key.shape[0], spare - 1), low)], 1
    )
    query_wide = jnp.concatenate(
        [query_t, jnp.ones((1, mine.shape[0]), low), jnp.zeros((spare - 1, mine.shape[0]), low)], 0
    )
    attended, mixed_out, log_total = attend(heads, query_wide, key_wide, value_t, rows)

    back = [mixed_out[0]] + [to_chip(mixed_out[d], -d) for d in range(1, chips)]
    twice = jnp.stack(back + back[:-1], 0)
    mixed_t = lax.dynamic_slice_in_dim(twice, (chips - chip) % chips, chips, 0)
    mixed_t = mixed_t.reshape(width, rows)
    projected = dot(mixed_t, out_full, tn) + bias_out
    hat_one, scale_one = normal_parts(tokens.astype(f32) + projected)
    first = hat_one * gain_first + shift_first
    first_low = first.astype(low)

    wide = jnp.concatenate(from_teams(first_low), 0)
    inner = dot(wide, up_part) + bias_up
    cdf = 0.5 * (1.0 + lax.erf(inner * 2.0**-0.5))
    slope = cdf + inner * (jnp.exp(-0.5 * inner * inner) * (2.0 * math.pi) ** -0.5)
    active_low = (inner * cdf).astype(low)
    active_low, slope = lax.optimization_barrier((active_low, slope))
    branch_part = dot(active_low, down_part)
    branch = return_teams(branch_part.reshape(teams, rows, width)) + bias_down
    hat_two, scale_two = normal_parts(first + branch)
    output = (hat_two * gain_second + shift_second).astype(low)
    grad_out = cotangent.astype(f32)
    grad_gain_two = jnp.sum(grad_out * hat_two, 0)
    grad_shift_two = jnp.sum(grad_out, 0)
    grad_second = normal_back(hat_two, scale_two, grad_out * gain_second)
    branch_grad = grad_second.astype(low)
    grad_b_down = jnp.sum(branch_grad.astype(f32), 0)
    wide_grad = jnp.concatenate(from_teams(branch_grad), 0)
    active_grad = dot(wide_grad, down_part, ((1,), (1,)))
    inner_grad = (active_grad * slope).astype(low)
    first_part = dot(inner_grad, up_part, ((1,), (1,)))
    first_grad = return_teams(first_part.reshape(teams, rows, width)) + grad_second
    grad_b_up = jnp.sum(inner_grad.astype(f32), 0)
    grad_down = dot(active_low, wide_grad, tn)
    grad_up = dot(wide, inner_grad, tn)

    grad_gain_one = jnp.sum(first_grad * hat_one, 0)
    grad_shift_one = jnp.sum(first_grad, 0)
    grad_first = normal_back(hat_one, scale_one, first_grad * gain_first)
    proj_grad = grad_first.astype(low)
    grad_b_out = jnp.sum(proj_grad.astype(f32), 0)
    mixed_grad_t = dot(out_full, proj_grad, ((1,), (1,))).astype(low)
    grad_out_w = dot(mixed_t, proj_grad)

    come = swap_chips(mixed_grad_t.reshape(chips, group, rows))
    grad_t = jnp.concatenate(come, 1)
    grad_rows = grad_t.T
    query_grad, key_sum, value_sum = attend_back(
        heads,
        rows,
        query_wide,
        query,
        key_wide,
        key_t,
        value,
        grad_t,
        grad_rows,
        attended,
        log_total,
    )
    half = mine.shape[0]
    pair = jnp.concatenate([key_sum, value_sum], 1)
    pair = pair[:half] + to_core(pair[half:].astype(low)).astype(f32)
    grads = jnp.concatenate([query_grad, pair.astype(low)], 1)
    token_part = dot(grads, w_heads, ((1,), (1,))).reshape(chips, rows, width)
    token_grad = grad_first + total(
        [token_part[0]] + [to_chip(token_part[d].astype(low), -d) for d in range(1, chips)]
    )
    grad_tokens = token_grad.astype(low)
    grad_heads = dot(mine, grads, tn)

    def cores_sum(terms, axis):
        away = to_core(pick(terms, 1 - core, axis).astype(low))
        return pick(terms, core, axis).astype(f32) + away.astype(f32)

    down_sum = cores_sum(grad_down.reshape(chips, 2, -1, width), 1).astype(low)
    out_down = total(swap_chips(down_sum))
    up_sum = cores_sum(grad_up.reshape(teams, chips, 2, part, quarter), 2).astype(low)
    up_sum = total(swap_chips(up_sum, 1)).astype(low)
    out_up = ordered(swap_teams(up_sum), team).transpose(1, 0, 2).reshape(part, hidden).astype(f32)
    out_sum = cores_sum(grad_out_w.reshape(teams, chips, 2, part, width), 2).astype(low)
    out_sum = total(swap_teams(out_sum)).astype(low)
    out_out = total(swap_chips(out_sum))

    def spread(piece, index, whole):
        return lax.dynamic_update_slice_in_dim(
            jnp.zeros((whole,), f32), piece, index * piece.shape[0], 0
        )

    grads_low = grads.astype(f32)
    grad_b_query = spread(jnp.sum(grads_low[:, :group], 0), chip, width)
    grad_b_value = spread(jnp.sum(grads_low[:, 2 * group :], 0), chip, width)
    grad_b_up = spread(grad_b_up, team, hidden)
    small = (
        grad_b_query,
        grad_b_value,
        grad_b_out,
        grad_gain_one,
        grad_shift_one,
        grad_b_down,
        grad_gain_two,
        grad_shift_two,
        grad_b_up,
    )
    small = jnp.concatenate([item.reshape(teams, chips, 2, 1, -1) for item in small], -1)
    small = jnp.pad(small, ((0, 0),) * 4 + ((0, 3 * group - small.shape[-1]),))
    blank = jnp.zeros((teams, chips, 2, held - part - 1, 3 * group), f32)
    terms = jnp.concatenate(
        [grad_heads.reshape(teams, chips, 2, part, 3 * group), small, blank], 3
    )
    terms = cores_sum(terms, 2).astype(low)
    terms = total(swap_teams(terms)).astype(low)
    found = ordered(swap_chips(terms), chip)
    matrices = found[:, :part].transpose(1, 0, 2).reshape(part, chips, 3, group).astype(f32)
    out_query, out_key, out_value = [matrices[:, :, i].reshape(part, width) for i in range(3)]
    vector_sum = jnp.sum(found[:, part].astype(f32), 0)
    vec = [vector_sum[i * part : (i + 1) * part] for i in range(8)]
    out_b_up = vector_sum[8 * part : 8 * part + b_up.shape[0]]
    return (
        output,
        grad_tokens,
        out_query,
        vec[0],
        out_key,
        out_value,
        vec[1],
        out_out,
        vec[2],
        vec[3],
        vec[4],
        out_up,
        out_b_up,
        out_down,
        vec[5],
        vec[6],
        vec[7],
    )


def solution(mesh):
    in_specs = (
        P(("batch", "ctx"), None),
        P("batch"),
        P(("batch", "ctx"), None),
        P(("batch", "ctx")),
        P(("batch", "ctx"), None),
        P(("batch", "ctx"), None),
        P(("batch", "ctx")),
        P(("batch", "ctx"), None),
        P(("batch", "ctx")),
        P(("batch", "ctx")),
        P(("batch", "ctx")),
        P(("batch", "ctx"), None),
        P(("batch", "ctx")),
        P(("batch", "ctx"), None),
        P(("batch", "ctx")),
        P(("batch", "ctx")),
        P(("batch", "ctx")),
        P(("batch", "ctx"), None),
    )
    out_specs = (
        P(("batch", "ctx"), None),
        P(("batch", "ctx"), None),
        P(("batch", "ctx"), None),
        P(("batch", "ctx")),
        P(("batch", "ctx"), None),
        P(("batch", "ctx"), None),
        P(("batch", "ctx")),
        P(("batch", "ctx"), None),
        P(("batch", "ctx")),
        P(("batch", "ctx")),
        P(("batch", "ctx")),
        P(("batch", "ctx"), None),
        P(("batch", "ctx")),
        P(("batch", "ctx"), None),
        P(("batch", "ctx")),
        P(("batch", "ctx")),
        P(("batch", "ctx")),
    )
    places = mesh.shape["ctx"]
    whole_heads = places % 2 == 0 and HEADS % (places // 2) == 0
    step = layer_split if whole_heads else body
    return jax.shard_map(step, mesh=mesh, in_specs=in_specs, out_specs=out_specs, check_vma=False)
```

```python
import functools
import math

import jax
import jax.numpy as jnp
from jax import lax
from jax.experimental import pallas as pl
from jax.experimental.pallas import tpu as pltpu
from jax.sharding import PartitionSpec as P

HEADS = 12
HEAD_DIM = 64


epsilon = 1e-06
masked_score = -1e30


def shifted(block, axis, distance):
    devices = range(lax.axis_size(axis))
    route = [((i - distance) % len(devices), i) for i in devices]
    return lax.ppermute(block, axis, route)


def normalize(resid, gain, shift):
    center = resid - jnp.mean(resid, -1, keepdims=True)
    spread = jnp.mean(center * center, -1, keepdims=True)
    return center * lax.rsqrt(spread + epsilon) * gain + shift


def gelu_exact(value):
    return jax.nn.gelu(value, approximate=False)


def head_scores(query_blk, key_blk, owner, length):
    count = key_blk.shape[0]
    raw = jnp.einsum(
        "qhd,khd->hqk",
        query_blk.reshape(-1, HEADS, HEAD_DIM),
        key_blk.reshape(count, HEADS, HEAD_DIM),
        preferred_element_type=jnp.float32,
    )
    position = owner * count + jnp.arange(count, dtype=jnp.int32)
    return jnp.where((position < length)[None, None, :], raw * HEAD_DIM ** (-0.5), masked_score)


def block_grads(query_blk, grad_blk, log_blk, delta_blk, key_blk, value_blk, owner, length):
    rows = query_blk.shape[0]
    count = key_blk.shape[0]
    scores = head_scores(query_blk, key_blk, owner, length)
    probs = jnp.exp(scores - log_blk[:, :, None])
    probs_low = probs.astype(jnp.bfloat16)
    grad_heads = grad_blk.reshape(rows, HEADS, HEAD_DIM)
    query_heads = query_blk.reshape(rows, HEADS, HEAD_DIM)
    key_heads = key_blk.reshape(count, HEADS, HEAD_DIM)
    value_heads = value_blk.reshape(count, HEADS, HEAD_DIM)
    prob_grad = jnp.einsum(
        "qhd,khd->hqk", grad_heads, value_heads, preferred_element_type=jnp.float32
    )
    score_grad = (probs * (prob_grad - delta_blk[:, :, None])).astype(jnp.bfloat16)
    value_term = jnp.einsum(
        "hqk,qhd->khd", probs_low, grad_heads, preferred_element_type=jnp.float32
    )
    key_term = jnp.einsum(
        "hqk,qhd->khd", score_grad, query_heads, preferred_element_type=jnp.float32
    ) * HEAD_DIM ** (-0.5)
    query_term = jnp.einsum(
        "hqk,khd->qhd", score_grad, key_heads, preferred_element_type=jnp.float32
    ) * HEAD_DIM ** (-0.5)
    return (
        query_term.reshape(rows, -1),
        key_term.reshape(count, -1),
        value_term.reshape(count, -1),
    )


def body(
    tokens,
    lengths,
    w_query,
    b_query,
    w_key,
    w_value,
    b_value,
    w_out,
    b_out,
    gain_one,
    shift_one,
    w_up,
    b_up,
    w_down,
    b_down,
    gain_two,
    shift_two,
    cotangent,
):
    cycle = lax.axis_size("ctx")
    place = lax.axis_index("ctx")
    length = lengths[0]
    rows = tokens.shape[0]
    width = tokens.shape[1]
    gathered = (
        lax.all_gather(w_query, ("batch", "ctx"), axis=0, tiled=True),
        lax.all_gather(w_key, ("batch", "ctx"), axis=0, tiled=True),
        lax.all_gather(w_value, ("batch", "ctx"), axis=0, tiled=True),
        lax.all_gather(w_out, ("batch", "ctx"), axis=0, tiled=True),
        lax.all_gather(w_up, ("batch", "ctx"), axis=0, tiled=True),
        lax.all_gather(w_down, ("batch", "ctx"), axis=0, tiled=True),
        lax.all_gather(b_query, ("batch", "ctx"), axis=0, tiled=True),
        lax.all_gather(b_value, ("batch", "ctx"), axis=0, tiled=True),
        lax.all_gather(b_out, ("batch", "ctx"), axis=0, tiled=True),
        lax.all_gather(gain_one, ("batch", "ctx"), axis=0, tiled=True),
        lax.all_gather(shift_one, ("batch", "ctx"), axis=0, tiled=True),
        lax.all_gather(b_up, ("batch", "ctx"), axis=0, tiled=True),
        lax.all_gather(b_down, ("batch", "ctx"), axis=0, tiled=True),
        lax.all_gather(gain_two, ("batch", "ctx"), axis=0, tiled=True),
        lax.all_gather(shift_two, ("batch", "ctx"), axis=0, tiled=True),
    )
    query_full, key_full, value_full, out_full, up_full, down_full = gathered[:6]
    small = [item.astype(jnp.float32) for item in gathered[6:]]
    (
        bias_query,
        bias_value,
        bias_out,
        gain_first,
        shift_first,
        bias_up,
        bias_down,
        gain_second,
        shift_second,
    ) = small
    query_low = (
        jnp.dot(tokens, query_full, preferred_element_type=jnp.float32) + bias_query
    ).astype(jnp.bfloat16)
    key_low = jnp.dot(tokens, key_full, preferred_element_type=jnp.float32).astype(jnp.bfloat16)
    value_low = (
        jnp.dot(tokens, value_full, preferred_element_type=jnp.float32) + bias_value
    ).astype(jnp.bfloat16)
    start_top = jnp.full((HEADS, rows), masked_score, jnp.float32)
    start_total = jnp.zeros((HEADS, rows), jnp.float32)
    start_sum = jnp.zeros((rows, HEADS, HEAD_DIM), jnp.float32)

    def running(state, pair, owner):
        top, total, summed = state
        scores = head_scores(query_low, pair[0], owner, length)
        new_top = jnp.maximum(top, jnp.max(scores, -1))
        factor = jnp.exp(top - new_top)
        expos = jnp.exp(scores - new_top[:, :, None])
        total = total * factor + jnp.sum(expos, -1)
        summed = summed * factor.T[:, :, None] + jnp.einsum(
            "hqk,khd->qhd",
            expos.astype(jnp.bfloat16),
            pair[1].reshape(-1, HEADS, HEAD_DIM),
            preferred_element_type=jnp.float32,
        )
        return (new_top, total, summed)

    def run_step(step, carry):
        pair, state = carry
        state = running(state, pair, (place - step) % cycle)
        pair = shifted((pair[0], pair[1]), "ctx", 1)
        return (pair, state)

    pair, state = lax.fori_loop(
        0, cycle - 1, run_step, ((key_low, value_low), (start_top, start_total, start_sum))
    )
    top, total, summed = running(state, pair, (place + 1) % cycle)
    log_total = top + jnp.log(total)
    attended = (summed / total.T[:, :, None]).reshape(rows, width)
    mixed = attended.astype(jnp.bfloat16)
    projected = jnp.dot(mixed, out_full, preferred_element_type=jnp.float32) + bias_out
    first, first_back = jax.vjp(
        normalize, tokens.astype(jnp.float32) + projected, gain_first, shift_first
    )
    first_low = first.astype(jnp.bfloat16)
    inner = jnp.dot(first_low, up_full, preferred_element_type=jnp.float32) + bias_up
    active, gelu_back = jax.vjp(gelu_exact, inner)
    active_low = active.astype(jnp.bfloat16)
    branch = jnp.dot(active_low, down_full, preferred_element_type=jnp.float32) + bias_down
    result, second_back = jax.vjp(normalize, first + branch, gain_second, shift_second)
    output = result.astype(jnp.bfloat16)
    query_back, key_back, value_back, out_back, up_back, down_back = (
        query_full,
        key_full,
        value_full,
        out_full,
        up_full,
        down_full,
    )
    grad_second, grad_gain_two, grad_shift_two = second_back(cotangent.astype(jnp.float32))
    branch_grad = grad_second.astype(jnp.bfloat16)
    grad_b_down = jnp.sum(branch_grad.astype(jnp.float32), 0)
    grad_w_down = jnp.einsum(
        "tf,td->fd", active_low, branch_grad, preferred_element_type=jnp.float32
    )
    active_grad = jnp.einsum(
        "td,fd->tf", branch_grad, down_back, preferred_element_type=jnp.float32
    )
    inner_grad = gelu_back(active_grad)[0].astype(jnp.bfloat16)
    grad_b_up = jnp.sum(inner_grad.astype(jnp.float32), 0)
    grad_w_up = jnp.einsum("td,tf->df", first_low, inner_grad, preferred_element_type=jnp.float32)
    first_grad = (
        jnp.einsum("tf,df->td", inner_grad, up_back, preferred_element_type=jnp.float32)
        + grad_second
    )
    grad_first, grad_gain_one, grad_shift_one = first_back(first_grad)
    proj_grad = grad_first.astype(jnp.bfloat16)
    grad_b_out = jnp.sum(proj_grad.astype(jnp.float32), 0)
    grad_w_out = jnp.einsum("td,te->de", mixed, proj_grad, preferred_element_type=jnp.float32)
    mixed_grad = jnp.einsum(
        "te,de->td", proj_grad, out_back, preferred_element_type=jnp.float32
    ).astype(jnp.bfloat16)
    delta = jnp.sum(
        (mixed_grad.astype(jnp.float32) * attended).reshape(rows, HEADS, HEAD_DIM), -1
    ).T
    zeros = jnp.zeros((rows, width), jnp.float32)

    def move_key_grads(grads):
        return (
            shifted(grads[0].astype(jnp.bfloat16), "ctx", 1).astype(jnp.float32),
            shifted(grads[1].astype(jnp.bfloat16), "ctx", 1).astype(jnp.float32),
        )

    def key_step(step, carry):
        blocks, grads, query_acc = carry
        query_term, key_term, value_term = block_grads(
            query_low,
            mixed_grad,
            log_total,
            delta,
            blocks[0],
            blocks[1],
            (place - step) % cycle,
            length,
        )
        grads = move_key_grads((grads[0] + key_term, grads[1] + value_term))
        blocks = shifted((blocks[0], blocks[1]), "ctx", 1)
        return (blocks, grads, query_acc + query_term)

    blocks, grads, query_acc = lax.fori_loop(
        0, cycle - 1, key_step, ((key_low, value_low), (zeros, zeros), zeros)
    )
    query_term, key_term, value_term = block_grads(
        query_low, mixed_grad, log_total, delta, blocks[0], blocks[1], (place + 1) % cycle, length
    )
    key_acc, value_acc = move_key_grads((grads[0] + key_term, grads[1] + value_term))
    query_acc = query_acc + query_term
    query_grad = query_acc.astype(jnp.bfloat16)
    key_grad = key_acc.astype(jnp.bfloat16)
    value_grad = value_acc.astype(jnp.bfloat16)
    grad_b_query = jnp.sum(query_grad.astype(jnp.float32), 0)
    grad_b_value = jnp.sum(value_grad.astype(jnp.float32), 0)
    grad_w_query = jnp.einsum("td,te->de", tokens, query_grad, preferred_element_type=jnp.float32)
    grad_w_key = jnp.einsum("td,te->de", tokens, key_grad, preferred_element_type=jnp.float32)
    grad_w_value = jnp.einsum("td,te->de", tokens, value_grad, preferred_element_type=jnp.float32)
    token_grad = grad_first + jnp.einsum(
        "te,de->td", query_grad, query_back, preferred_element_type=jnp.float32
    )
    token_grad = token_grad + jnp.einsum(
        "te,de->td", key_grad, key_back, preferred_element_type=jnp.float32
    )
    token_grad = token_grad + jnp.einsum(
        "te,de->td", value_grad, value_back, preferred_element_type=jnp.float32
    )
    grad_tokens = token_grad.astype(jnp.bfloat16)
    sharded = (
        lax.psum_scatter(grad_w_query, ("batch", "ctx"), scatter_dimension=0, tiled=True),
        lax.psum_scatter(grad_b_query, ("batch", "ctx"), scatter_dimension=0, tiled=True),
        lax.psum_scatter(grad_w_key, ("batch", "ctx"), scatter_dimension=0, tiled=True),
        lax.psum_scatter(grad_w_value, ("batch", "ctx"), scatter_dimension=0, tiled=True),
        lax.psum_scatter(grad_b_value, ("batch", "ctx"), scatter_dimension=0, tiled=True),
        lax.psum_scatter(grad_w_out, ("batch", "ctx"), scatter_dimension=0, tiled=True),
        lax.psum_scatter(grad_b_out, ("batch", "ctx"), scatter_dimension=0, tiled=True),
        lax.psum_scatter(grad_gain_one, ("batch", "ctx"), scatter_dimension=0, tiled=True),
        lax.psum_scatter(grad_shift_one, ("batch", "ctx"), scatter_dimension=0, tiled=True),
        lax.psum_scatter(grad_w_up, ("batch", "ctx"), scatter_dimension=0, tiled=True),
        lax.psum_scatter(grad_b_up, ("batch", "ctx"), scatter_dimension=0, tiled=True),
        lax.psum_scatter(grad_w_down, ("batch", "ctx"), scatter_dimension=0, tiled=True),
        lax.psum_scatter(grad_b_down, ("batch", "ctx"), scatter_dimension=0, tiled=True),
        lax.psum_scatter(grad_gain_two, ("batch", "ctx"), scatter_dimension=0, tiled=True),
        lax.psum_scatter(grad_shift_two, ("batch", "ctx"), scatter_dimension=0, tiled=True),
    )
    return (
        output,
        grad_tokens,
        sharded[0],
        sharded[1],
        sharded[2],
        sharded[3],
        sharded[4],
        sharded[5],
        sharded[6],
        sharded[7],
        sharded[8],
        sharded[9],
        sharded[10],
        sharded[11],
        sharded[12],
        sharded[13],
        sharded[14],
    )


def normal_parts(resid):
    center = resid - jnp.mean(resid, -1, keepdims=True)
    spread = jnp.mean(center * center, -1, keepdims=True)
    scale = lax.rsqrt(spread + epsilon)
    return center * scale, scale


def normal_back(hat, scale, grad):
    inner = jnp.mean(grad * hat, -1, keepdims=True)
    return scale * (grad - jnp.mean(grad, -1, keepdims=True) - hat * inner)


def dot(left, right, dims=((1,), (0,))):
    return lax.dot_general(left, right, (dims, ((), ())), preferred_element_type=jnp.float32)


def head_rows(block, head, extra):
    row = lax.broadcasted_iota(jnp.int32, block.shape, 0)
    keep = (row >= head * HEAD_DIM) & (row < (head + 1) * HEAD_DIM)
    if extra:
        keep = keep | (row >= extra)
    return jnp.where(keep, block, jnp.zeros_like(block))


def head_lanes(block, head):
    lane = lax.broadcasted_iota(jnp.int32, block.shape, 1)
    keep = (lane >= head * HEAD_DIM) & (lane < (head + 1) * HEAD_DIM)
    return jnp.where(keep, block, jnp.zeros_like(block))


def copied_kernel(kernel, first, far, count, shapes, *refs):
    operands, refs = refs[:count], refs[count:]
    results, refs = refs[: len(shapes)], refs[len(shapes) :]
    moved = [i for i in range(count) if i >= first and i not in far]
    taken, refs = refs[: len(moved)], refs[len(moved) :]
    given, refs = refs[: len(shapes)], refs[len(shapes) :]
    coming, going, rest = refs[0], refs[1], refs[2:]
    local = list(operands)
    copies = []
    for index, at in enumerate(moved):
        copies.append(pltpu.make_async_copy(operands[at], taken[index], coming.at[index]))
        local[at] = taken[index]
    for copy in copies:
        copy.start()
    for copy in copies:
        copy.wait()
    copies = [
        pltpu.make_async_copy(given[index], results[index], going.at[index])
        for index in range(len(shapes))
    ]
    kernel(*local, *given, *rest, leave=lambda *which: [copies[index].start() for index in which])
    for copy in copies:
        copy.wait()


def one_step(
    kernel, operands, shapes, flops, name, first=1, far=(), scratch=(), exps=0, limit=14
):
    specs = []
    for index in range(len(operands)):
        if index < first:
            specs.append(pl.BlockSpec(memory_space=pltpu.SMEM))
        elif index in far:
            specs.append(pl.BlockSpec(memory_space=pl.ANY))
        else:
            specs.append(pl.BlockSpec(memory_space=pltpu.HBM))
    moved = [
        pltpu.VMEM(operand.shape, operand.dtype)
        for index, operand in enumerate(operands)
        if index >= first and index not in far
    ]
    given = [pltpu.VMEM(*shape) for shape in shapes]
    return pl.pallas_call(
        functools.partial(copied_kernel, kernel, first, far, len(operands), shapes),
        in_specs=specs,
        out_specs=[pl.BlockSpec(memory_space=pltpu.HBM)] * len(shapes),
        out_shape=[pltpu.HBM(*shape) for shape in shapes],
        scratch_shapes=moved
        + given
        + [pltpu.SemaphoreType.DMA((len(moved),)), pltpu.SemaphoreType.DMA((len(shapes),))]
        + list(scratch),
        compiler_params=pltpu.CompilerParams(vmem_limit_bytes=limit * 2**20),
        cost_estimate=pl.CostEstimate(
            flops=flops,
            bytes_accessed=sum(operand.size * operand.dtype.itemsize for operand in operands),
            transcendentals=exps,
        ),
        name=name,
    )(*operands)


def turn(block):
    return jnp.transpose(block.astype(jnp.float32)).astype(block.dtype)


def attend_kernel(heads, chips, places, *refs, leave):
    own, others = refs[:chips], refs[chips : 2 * chips]
    weight, bias_query, bias_value = refs[2 * chips : 2 * chips + 3]
    refs = refs[2 * chips + 3 :]
    mine_ref, query, key, value, att, log = refs[:6]
    sent, (every, query_t, value_t, mixed) = refs[6 : 6 + chips], refs[6 + chips :]
    low, f32 = jnp.bfloat16, jnp.float32
    width = heads * HEAD_DIM
    count, rows, depth = every.shape
    spare = key.shape[1] - width

    for distance in range(chips):
        slot = lax.rem(places[0] - distance + chips, chips)
        every[slot] = own[distance][:rows, :]
        every[chips + slot] = others[distance][:rows, :]
    tokens = every[...].reshape(count * rows, depth)
    mine = chips * rows
    mine_ref[...] = tokens[:mine]
    first = dot(tokens[:mine], weight[:, :width]) + bias_query[...]
    first = (first.astype(low).astype(f32) * HEAD_DIM ** (-0.5)).astype(low)
    query[...] = first
    one = lax.broadcasted_iota(jnp.int32, (spare, mine), 0) == 0
    query_t[...] = jnp.concatenate([turn(first), jnp.where(one, 1.0, 0.0).astype(low)], 0)
    second = dot(tokens, weight[:, width : 2 * width]).astype(low)
    row = lax.broadcasted_iota(jnp.int32, (rows, spare), 0)
    lane = lax.broadcasted_iota(jnp.int32, (rows, spare), 1)
    for block in range(count):
        hide = jnp.where((row < places[1 + block]) | (lane > 0), 0.0, masked_score)
        at = slice(block * rows, (block + 1) * rows)
        key[at, :] = jnp.concatenate([second[at].astype(f32), hide], 1).astype(low)
    third = (dot(tokens, weight[:, 2 * width :]) + bias_value[...]).astype(low)
    value[...] = third
    value_t[...] = turn(third)
    leave(0, 1, 2, 3)

    pieces = 2 if chips % 2 == 0 else 1
    for step in range(chips // pieces):
        span = slice(step * pieces * rows, (step + 1) * pieces * rows)
        for head in range(heads):
            scores = dot(key[...], head_rows(query_t[:, span], head, width))
            top = jnp.max(scores, 0, keepdims=True)
            expos = jnp.exp(scores - top)
            total = jnp.sum(expos, 0, keepdims=True)
            at = slice(head * HEAD_DIM, (head + 1) * HEAD_DIM)
            summed = dot(value_t[at, :], expos.astype(low)) / total
            att[at, span] = summed
            for piece in range(pieces):
                mixed[step * pieces + piece, at, :] = summed[
                    :, piece * rows : (piece + 1) * rows
                ].astype(low)
            log[head : head + 1, span] = top + jnp.log(total)
    for distance in range(chips):
        sent[distance][...] = mixed[lax.rem(places[0] + distance, chips)]
    leave(*range(4, 6 + chips))


def attend(heads, places, own, others, weight, bias_query, bias_value):
    chips = len(own)
    rows, depth = own[0].shape
    count = 2 * chips
    mine, keys = chips * rows, count * rows
    width = heads * HEAD_DIM
    wide = -(-(width + 1) // 128) * 128
    low, f32 = jnp.bfloat16, jnp.float32
    return one_step(
        functools.partial(attend_kernel, heads, chips),
        [places, *own, *others, weight, bias_query, bias_value],
        [
            ((mine, depth), low),
            ((mine, width), low),
            ((keys, wide), low),
            ((keys, width), low),
            ((width, mine), f32),
            ((heads, mine), f32),
        ]
        + [((width, rows), low)] * chips,
        flops=4 * heads * mine * keys * 256 + 6 * keys * depth * width,
        name="attend",
        scratch=[
            pltpu.VMEM((count, rows, depth), low),
            pltpu.VMEM((wide, mine), low),
            pltpu.VMEM((width, keys), low),
            pltpu.VMEM((chips, width, rows), low),
        ],
        exps=heads * mine * keys,
    )


def attend_back_kernel(heads, chips, places, query, key, value, att, log, *refs, leave):
    come_refs, refs = refs[:chips], refs[chips + 1 :]
    query_grad, kept, away, key_sum, value_sum, grad_t, query_t, key_t = refs
    low = jnp.bfloat16
    width, rows = come_refs[0].shape
    mine = chips * rows
    for distance in range(chips):
        slot = lax.rem(places[0] - distance + chips, chips)
        grad_t[slot] = come_refs[distance][...]
    one = lax.broadcasted_iota(jnp.int32, (key.shape[1] - width, mine), 0) == 0
    query_t[...] = jnp.concatenate([turn(query[...]), jnp.where(one, 1.0, 0.0).astype(low)], 0)
    key_t[...] = turn(key[:, :width])
    pieces = 2 if chips % 2 == 0 else 1
    for step in range(chips // pieces):
        span = slice(step * pieces * rows, (step + 1) * pieces * rows)
        come = jnp.concatenate([grad_t[step * pieces + piece] for piece in range(pieces)], 1)
        come_rows = turn(come)
        turned = []
        for head in range(heads):
            at = slice(head * HEAD_DIM, (head + 1) * HEAD_DIM)
            scores = dot(key[...], head_rows(query_t[:, span], head, width))
            probs = jnp.exp(scores - log[head : head + 1, span])
            prob_grad = dot(value[...], head_rows(come, head, 0))
            delta = jnp.sum(come[at].astype(jnp.float32) * att[at, span], 0, keepdims=True)
            score_grad = (probs * (prob_grad - delta)).astype(low)
            turned.append(dot(key_t[at, :], score_grad))
            key_term = dot(score_grad, head_lanes(query[span, :], head))
            value_term = dot(probs.astype(low), head_lanes(come_rows, head))
            if step == 0 and head == 0:
                key_sum[...] = key_term
                value_sum[...] = value_term
            else:
                key_sum[...] += key_term
                value_sum[...] += value_term
        gathered = jnp.concatenate(turned, 0) * HEAD_DIM ** (-0.5)
        query_grad[span, :] = jnp.transpose(gathered).astype(low)
    kept[...] = jnp.concatenate([key_sum[:mine, :], value_sum[:mine, :]], 1)
    away[...] = jnp.concatenate([key_sum[mine:, :], value_sum[mine:, :]], 1).astype(low)
    leave(0, 1, 2)


def attend_back(heads, places, query, key, value, att, log, come, marker):
    chips = len(come)
    mine, width = query.shape
    keys, wide = key.shape
    low, f32 = jnp.bfloat16, jnp.float32
    return one_step(
        functools.partial(attend_back_kernel, heads, chips),
        [places, query, key, value, att, log, *come, marker],
        [((mine, width), low), ((mine, 2 * width), f32), ((keys - mine, 2 * width), low)],
        flops=10 * heads * mine * keys * 256,
        name="attend_back",
        far=(6 + chips,),
        scratch=[
            pltpu.VMEM((keys, width), f32),
            pltpu.VMEM((keys, width), f32),
            pltpu.VMEM((chips, width, mine // chips), low),
            pltpu.VMEM((wide, mine), low),
            pltpu.VMEM((width, keys), low),
        ],
        exps=heads * mine * keys,
    )


def finish_kernel(
    chips, places, mine, weight, query_grad, kept, come, short, *refs, leave
):
    low, f32 = jnp.bfloat16, jnp.float32
    sent, (own_terms, away_terms, terms, blocks) = refs[:chips], refs[chips:]
    owners, _, part, width = terms.shape
    pair = (kept[...] + come[...].astype(f32)).astype(low)
    grads = jnp.concatenate([query_grad[...].astype(f32), pair.astype(f32)], 1)
    sums = jnp.sum(grads, 0, keepdims=True)
    grads = grads.astype(low)
    part_grad = dot(grads, weight[...], ((1,), (1,))).astype(low)
    blocks[...] = part_grad.reshape(blocks.shape)
    for distance in range(chips):
        sent[distance][...] = blocks[lax.rem(places[0] + distance, chips)]
        leave(distance)
    terms[...] = dot(mine[...], grads, ((0,), (0,))).reshape(terms.shape)
    core = places[1]
    count = short.shape[2]
    row = lax.broadcasted_iota(jnp.int32, (count, width), 0)
    below = jnp.where(row == count - 1, sums, 0.0)
    for index, ref, which in ((1, away_terms, 1 - core), (0, own_terms, core)):
        for owner in range(owners):
            block = [terms[owner, which], short[owner, which] + below]
            ref[owner] = jnp.concatenate(block, 0).astype(ref.dtype)
        leave(chips + index)


def finish(chips, places, mine, weight, query_grad, kept, come, short):
    count, depth = mine.shape
    width = weight.shape[1]
    owners = short.shape[0]
    part = depth // (2 * owners)
    held = part + short.shape[2]
    block = (count // chips, depth)
    return one_step(
        functools.partial(finish_kernel, chips),
        [places, mine, weight, query_grad, kept, come, short],
        [
            *[(block, jnp.bfloat16)] * chips,
            ((owners, held, width), jnp.float32),
            ((owners, held, width), jnp.bfloat16),
        ],
        flops=4 * count * depth * width,
        name="finish",
        scratch=[
            pltpu.VMEM((owners, 2, part, width), jnp.float32),
            pltpu.VMEM((chips, *block), jnp.bfloat16),
        ],
    )


def bundle_kernel(own, come, w_out, w_up, out, leave):
    f32 = jnp.float32
    teams, chips, part, width = w_out.shape
    owners, held, group = own.shape
    for team in range(teams):
        for chip in range(chips):
            owner = team * chips + chip
            block = own[owner] + come[owner].astype(f32)
            block = jnp.pad(block, ((0, 0), (0, width - group)))
            start = chip * (held + part)
            both = jnp.concatenate([block, w_out[team, chip].astype(f32)], 0)
            out[team, start : start + held + part] = both.astype(out.dtype)
        out[team, chips * (held + part) :] = w_up[team]
    leave(0)


def bundle(own, come, w_out, w_up):
    teams, chips, part, width = w_out.shape
    held = own.shape[1]
    shape = (teams, chips * (held + part) + part, width)
    return one_step(
        bundle_kernel,
        [own, come, w_out, w_up],
        [(shape, jnp.bfloat16)],
        flops=0,
        limit=8,
        name="bundle",
        first=0,
    )[0]


def unpack_kernel(part, group, found, *outs, leave):
    chips, count, _ = found.shape
    blocks = [found[chip].astype(jnp.float32) for chip in range(chips)]
    for index in range(3):
        columns = slice(index * group, (index + 1) * group)
        outs[index][...] = jnp.concatenate([block[:part, columns] for block in blocks], 1)
    total = blocks[0]
    for block in blocks[1:]:
        total = total + block
    outs[3][...] = total[count - part :]
    outs[4][...] = total[part : count - part]
    outs[5][...] = jnp.concatenate([b[count - part - 1 : count - part] for b in blocks], 0)
    leave(*range(6))


def unpack(part, group, found):
    chips, count, width = found.shape
    shapes = [((part, width), jnp.float32)] * 4
    shapes.append(((count - 2 * part, width), jnp.float32))
    shapes.append(((chips, width), jnp.float32))
    return one_step(
        functools.partial(unpack_kernel, part, group),
        [found],
        shapes,
        flops=found.size,
        limit=8,
        name="unpack",
        first=0,
    )


def wait_kernel(*refs):
    pass


def after(block, *others):
    anywhere = pl.BlockSpec(memory_space=pl.ANY)
    return pl.pallas_call(
        wait_kernel,
        in_specs=[anywhere] * (1 + len(others)),
        out_specs=anywhere,
        out_shape=jax.ShapeDtypeStruct(block.shape, block.dtype),
        input_output_aliases={0: 0},
        compiler_params=pltpu.CompilerParams(vmem_limit_bytes=2**20),
        name="after",
    )(block, *others)


def lay_kernel(tokens, w_out, both):
    both[...] = jnp.concatenate([tokens[...], w_out[...]], 0)


def lay(tokens, w_out):
    shape = (tokens.shape[0] + w_out.shape[0], tokens.shape[1])
    return pl.pallas_call(
        lay_kernel,
        in_specs=[pl.BlockSpec(memory_space=pltpu.VMEM)] * 2,
        out_specs=pl.BlockSpec(memory_space=pltpu.VMEM),
        out_shape=jax.ShapeDtypeStruct(shape, tokens.dtype),
        name="lay",
    )(tokens, w_out)


def pack_kernel(chips, w_query, w_key, w_value, vectors, b_up, out):
    part = w_query.shape[0]
    group = w_query.shape[1] // chips
    count = vectors.shape[0]
    rest = out.shape[1] - part
    short = jnp.concatenate(
        [
            jnp.pad(vectors[...].astype(jnp.float32), ((0, rest - count), (0, 128 - part))),
            jnp.pad(
                b_up[...].astype(jnp.float32),
                ((0, rest - 1), (0, 3 * group - 128 - b_up.shape[1])),
            ),
        ],
        1,
    )
    for index in range(chips):
        columns = slice(index * group, (index + 1) * group)
        block = jnp.concatenate(
            [item[:, columns].astype(jnp.float32) for item in (w_query, w_key, w_value)], 1
        )
        both = jnp.concatenate([block, short], 0)
        spare = out.shape[2] - both.shape[1]
        out[index] = jnp.pad(both, ((0, 0), (0, spare))).astype(jnp.bfloat16)


def pack(chips, w_query, w_key, w_value, vectors, b_up, held):
    part, width = w_query.shape
    return pl.pallas_call(
        functools.partial(pack_kernel, chips),
        in_specs=[pl.BlockSpec(memory_space=pltpu.VMEM)] * 5,
        out_specs=pl.BlockSpec(memory_space=pltpu.VMEM),
        out_shape=jax.ShapeDtypeStruct((chips, held, width), jnp.bfloat16),
        name="pack",
    )(w_query, w_key, w_value, vectors, b_up)


def share_kernel(packed, w_up, out):
    teams, count, width = out.shape
    chips, held, _ = packed.shape
    for team in range(teams):
        for chip in range(chips):
            out[team, chip * held : (chip + 1) * held] = packed[chip]
        out[team, chips * held :] = w_up[:, team * width : (team + 1) * width]


def share(teams, packed, w_up):
    chips, held, width = packed.shape
    part, hidden = w_up.shape
    return pl.pallas_call(
        share_kernel,
        in_specs=[pl.BlockSpec(memory_space=pltpu.VMEM)] * 2,
        out_specs=pl.BlockSpec(memory_space=pltpu.VMEM),
        out_shape=jax.ShapeDtypeStruct(
            (teams, chips * held + part, hidden // teams), jnp.bfloat16
        ),
        name="share",
    )(packed, w_up)


def pick(blocks, index, axis=0):
    return lax.dynamic_index_in_dim(blocks, index, axis, keepdims=False)


def ordered(found, me):
    count = len(found)
    rising = [found[count - 1 - i] for i in range(count)]
    twice = jnp.stack(rising + rising[:-1], 0)
    return lax.dynamic_slice_in_dim(twice, count - 1 - me, count, 0)


def layer_split(
    tokens,
    lengths,
    w_query,
    b_query,
    w_key,
    w_value,
    b_value,
    w_out,
    b_out,
    gain_one,
    shift_one,
    w_up,
    b_up,
    w_down,
    b_down,
    gain_two,
    shift_two,
    cotangent,
):
    f32, low = jnp.float32, jnp.bfloat16
    teams = lax.axis_size("batch")
    chips = lax.axis_size("ctx") // 2
    team = lax.axis_index("batch")
    place = lax.axis_index("ctx")
    chip, core = place // 2, place % 2
    rows, width = tokens.shape
    part = w_query.shape[0]
    hidden = w_up.shape[1]
    quarter = hidden // teams
    heads = HEADS // chips
    group = heads * HEAD_DIM
    length = lengths[0]

    def to_chip(block, distance):
        route = [(i, (i // 2 + distance) % chips * 2 + i % 2) for i in range(2 * chips)]
        return lax.ppermute(block, "ctx", route)

    def to_core(block):
        return lax.ppermute(block, "ctx", [(i, i ^ 1) for i in range(2 * chips)])

    def to_team(block, distance):
        return lax.ppermute(block, "batch", [(i, (i + distance) % teams) for i in range(teams)])

    def from_chips(block):
        return [block] + [to_chip(block, d) for d in range(1, chips)]

    def from_teams(block):
        return [block] + [to_team(block, d) for d in range(1, teams)]

    def swap_chips(blocks, axis=0):
        return [pick(blocks, chip, axis)] + [
            to_chip(pick(blocks, (chip + d) % chips, axis), d) for d in range(1, chips)
        ]

    def swap_teams(blocks, axis=0):
        return [pick(blocks, team, axis)] + [
            to_team(pick(blocks, (team + d) % teams, axis), d) for d in range(1, teams)
        ]

    same_core = [[2 * z + c for z in range(chips)] for c in range(2)]

    def trade_chips(blocks):
        return lax.all_to_all(blocks, "ctx", 0, 0, axis_index_groups=same_core)

    def trade_teams(blocks):
        return lax.all_to_all(blocks, "batch", 0, 0)

    def both_cores(block, axis):
        other = to_core(block)
        first = jnp.where(core == 0, block, other)
        second = jnp.where(core == 0, other, block)
        return jnp.stack([first, second], axis)

    def cores_sum(terms, axis):
        away = to_core(pick(terms, 1 - core, axis).astype(low))
        return pick(terms, core, axis).astype(f32) + away.astype(f32)

    def total(blocks):
        result = blocks[0].astype(f32)
        for block in blocks[1:]:
            result = result + block.astype(f32)
        return result

    def return_teams(blocks):
        return total(
            [blocks[0]] + [to_team(blocks[d].astype(low), -d) for d in range(1, teams)]
        )

    vectors = (
        b_query,
        b_value,
        b_out,
        gain_one,
        shift_one,
        b_down,
        gain_two,
        shift_two,
    )
    held = -(-(part + len(vectors)) // 16) * 16
    laid = lay(tokens, w_out)
    packed = pack(
        chips,
        w_query,
        w_key,
        w_value,
        jnp.stack(vectors),
        b_up[None],
        held,
    )
    packed = trade_chips(packed)
    pieces = from_chips(after(laid, packed))
    traded = trade_teams(share(teams, packed, w_up))
    up_blocks = traded[:, chips * held :]
    packed = both_cores(traded[:, : chips * held].reshape(teams, chips, held, width), 2)
    w_heads = packed[:, :, :, :part, : 3 * group].reshape(width, 3 * group)
    shorts = packed[:, :, :, part:].reshape(teams * chips * 2, held - part, width)

    rows_of = shorts[:, :, :part].transpose(1, 0, 2).reshape(held - part, width)
    bias_query, bias_value, bias_out, gain_first, shift_first = rows_of[:5].astype(f32)
    bias_down, gain_second, shift_second = rows_of[5:8].astype(f32)
    bias_up = shorts[:, 0, 128 : 128 + b_up.shape[0]].reshape(-1).astype(f32)
    bias_up = lax.dynamic_slice_in_dim(bias_up, team * quarter, quarter)
    bias_query = lax.dynamic_slice_in_dim(bias_query, chip * group, group)
    bias_value = lax.dynamic_slice_in_dim(bias_value, chip * group, group)

    others = [to_core(tokens)] + [to_core(piece) for piece in pieces[1:]]
    starts = jnp.arange(chips, dtype=jnp.int32) * (2 * rows)
    starts = jnp.concatenate([starts + core * rows, starts + (1 - core) * rows])
    places = jnp.concatenate([chip[None], length - starts])

    out_rel = [w_out] + [piece[rows:] for piece in pieces[1:]]
    later = jnp.concatenate([up_blocks.reshape(teams * part, quarter), w_down], 0)
    later = lax.all_gather(later, "ctx", axis=0)
    out_blocks = after(ordered(out_rel, chip), w_heads)
    out_blocks = trade_teams(jnp.broadcast_to(out_blocks[None], (teams,) + out_blocks.shape))

    mine, query, key, value, attended, log_total, *mixed_out = attend(
        heads,
        places,
        [tokens] + pieces[1:],
        others,
        w_heads,
        bias_query[None],
        bias_value[None],
    )
    up_part = later[:, : teams * part].reshape(2 * chips, teams, part, quarter)
    up_part = up_part.transpose(1, 0, 2, 3).reshape(width, quarter)
    down_part = later[:, teams * part :].reshape(quarter, width)
    out_full = both_cores(after(out_blocks, log_total), 2).reshape(width, width)

    tn = ((0,), (0,))
    mixed_rel = [mixed_out[0]] + [to_chip(mixed_out[d], d) for d in range(1, chips)]
    mixed_t = ordered(mixed_rel, chip).reshape(width, rows)
    projected = dot(mixed_t, out_full, tn) + bias_out
    hat_one, scale_one = normal_parts(tokens.astype(f32) + projected)
    first = hat_one * gain_first + shift_first
    first_low = first.astype(low)

    wide = jnp.concatenate(from_teams(first_low), 0)
    inner = dot(wide, up_part) + bias_up
    cdf = 0.5 * (1.0 + lax.erf(inner * 2.0**-0.5))
    slope = cdf + inner * (jnp.exp(-0.5 * inner * inner) * (2.0 * math.pi) ** -0.5)
    active_low = (inner * cdf).astype(low)
    active_low, slope = lax.optimization_barrier((active_low, slope))
    branch_part = dot(active_low, down_part)
    branch = return_teams(branch_part.reshape(teams, rows, width)) + bias_down
    hat_two, scale_two = normal_parts(first + branch)
    output = (hat_two * gain_second + shift_second).astype(low)
    grad_out = cotangent.astype(f32)
    grad_gain_two = jnp.sum(grad_out * hat_two, 0)
    grad_shift_two = jnp.sum(grad_out, 0)
    grad_second = normal_back(hat_two, scale_two, grad_out * gain_second)
    branch_grad = grad_second.astype(low)
    grad_b_down = jnp.sum(branch_grad.astype(f32), 0)
    wide_grad = jnp.concatenate(from_teams(branch_grad), 0)
    active_grad = dot(wide_grad, down_part, ((1,), (1,)))
    inner_grad = (active_grad * slope).astype(low)
    first_part = dot(inner_grad, up_part, ((1,), (1,))).astype(low)
    first_part = first_part.reshape(teams, rows, width)
    leaving = [first_part[d] for d in range(teams)]
    come_back = [to_team(leaving[d], -d) for d in range(1, teams)]
    first_grad = total([leaving[0]] + come_back) + grad_second
    grad_b_up = jnp.sum(inner_grad.astype(f32), 0)
    grad_down = dot(active_low, after(wide_grad, leaving[1]), tn)
    grad_up = dot(wide, after(inner_grad, leaving[1]), tn)

    grad_gain_one = jnp.sum(first_grad * hat_one, 0)
    grad_shift_one = jnp.sum(first_grad, 0)
    grad_first = normal_back(hat_one, scale_one, first_grad * gain_first)
    proj_grad = grad_first.astype(low)
    grad_b_out = jnp.sum(proj_grad.astype(f32), 0)
    mixed_grad_t = dot(out_full, proj_grad, ((1,), (1,))).astype(low)
    mixed_grad_t = mixed_grad_t.reshape(chips, group, rows)
    leaving = [pick(mixed_grad_t, (chip + d) % chips) for d in range(chips)]
    grad_out_w = dot(mixed_t, after(proj_grad, leaving[1]))
    out_sum = cores_sum(grad_out_w.reshape(teams, chips, 2, part, width), 2).astype(low)

    come = [leaving[0]] + [to_chip(leaving[d], d) for d in range(1, chips)]
    query_grad, kept, away = attend_back(
        heads, places, query, key, value, attended, log_total, come, out_sum
    )
    up_terms = grad_up.astype(low).reshape(teams, 2 * chips, part, quarter)
    up_terms = up_terms.transpose(1, 0, 2, 3).reshape(2 * chips, teams * part, quarter)
    down_terms = grad_down.astype(low).reshape(2 * chips, -1, width)
    sums = lax.psum_scatter(
        jnp.concatenate([up_terms, down_terms], 1), "ctx", scatter_dimension=0, tiled=False
    )
    up_sum = sums[: teams * part].reshape(teams, part, quarter)

    small = (
        grad_b_out,
        grad_gain_one,
        grad_shift_one,
        grad_b_down,
        grad_gain_two,
        grad_shift_two,
    )
    small = jnp.stack([item.reshape(teams * chips, 2, part) for item in small], 2)
    small = jnp.pad(small, ((0, 0),) * 2 + ((0, held - part - len(vectors) + 2), (0, 128 - part)))
    tall = lax.dynamic_update_slice_in_dim(
        jnp.zeros((hidden,), f32), grad_b_up, team * quarter, 0
    ).reshape(teams * chips, 2, 1, -1)
    lanes = 3 * group - 128 - tall.shape[-1]
    tall = jnp.pad(tall, ((0, 0),) * 2 + ((0, held - part - 1), (0, lanes)))
    *token_part, own_terms, away_terms = finish(
        chips,
        jnp.stack([chip, core]),
        mine,
        w_heads,
        query_grad,
        kept,
        to_core(away),
        jnp.concatenate([small, tall], 3),
    )
    token_come = [to_chip(token_part[d], d) for d in range(1, chips)]
    token_grad = grad_first + total([token_part[0]] + token_come)
    grad_tokens = token_grad.astype(low)

    traded = bundle(own_terms, to_core(away_terms), out_sum, up_sum)
    traded = trade_teams(traded)
    out_up = traded[:, -part:].transpose(1, 0, 2).reshape(part, hidden).astype(f32)
    terms = jnp.sum(traded[:, :-part].astype(f32), 0).astype(low)
    out_down = after(sums, traded)[teams * part :].astype(f32)
    found = trade_chips(after(terms.reshape(chips, held + part, width), grad_tokens))
    out_query, out_key, out_value, out_out, short_sum, sums = unpack(part, group, found)
    vec = [short_sum[i, :part] for i in range(6)]
    out_b_up = short_sum[0, 128 : 128 + b_up.shape[0]]
    own_sums = lax.dynamic_slice(sums, (team, 0), (1, 3 * group))[0].reshape(3, group)
    own_sums = lax.dynamic_slice(own_sums, (0, place * part), (3, part))
    return (
        output,
        grad_tokens,
        out_query,
        own_sums[0],
        out_key,
        out_value,
        own_sums[2],
        out_out,
        vec[0],
        vec[1],
        vec[2],
        out_up,
        out_b_up,
        out_down,
        vec[3],
        vec[4],
        vec[5],
    )


def solution(mesh):
    in_specs = (
        P(("batch", "ctx"), None),
        P("batch"),
        P(("batch", "ctx"), None),
        P(("batch", "ctx")),
        P(("batch", "ctx"), None),
        P(("batch", "ctx"), None),
        P(("batch", "ctx")),
        P(("batch", "ctx"), None),
        P(("batch", "ctx")),
        P(("batch", "ctx")),
        P(("batch", "ctx")),
        P(("batch", "ctx"), None),
        P(("batch", "ctx")),
        P(("batch", "ctx"), None),
        P(("batch", "ctx")),
        P(("batch", "ctx")),
        P(("batch", "ctx")),
        P(("batch", "ctx"), None),
    )
    out_specs = (
        P(("batch", "ctx"), None),
        P(("batch", "ctx"), None),
        P(("batch", "ctx"), None),
        P(("batch", "ctx")),
        P(("batch", "ctx"), None),
        P(("batch", "ctx"), None),
        P(("batch", "ctx")),
        P(("batch", "ctx"), None),
        P(("batch", "ctx")),
        P(("batch", "ctx")),
        P(("batch", "ctx")),
        P(("batch", "ctx"), None),
        P(("batch", "ctx")),
        P(("batch", "ctx"), None),
        P(("batch", "ctx")),
        P(("batch", "ctx")),
        P(("batch", "ctx")),
    )
    places = mesh.shape["ctx"]
    whole_heads = places % 2 == 0 and HEADS % (places // 2) == 0
    step = layer_split if whole_heads else body
    return jax.shard_map(step, mesh=mesh, in_specs=in_specs, out_specs=out_specs, check_vma=False)
```

```python
import functools
import math

import jax
import jax.numpy as jnp
from jax import lax
from jax.experimental import pallas as pl
from jax.experimental.pallas import tpu as pltpu
from jax.sharding import PartitionSpec as P

HEADS = 12
HEAD_DIM = 64


epsilon = 1e-06
masked_score = -1e30


def shifted(block, axis, distance):
    devices = range(lax.axis_size(axis))
    route = [((i - distance) % len(devices), i) for i in devices]
    return lax.ppermute(block, axis, route)


def normalize(resid, gain, shift):
    center = resid - jnp.mean(resid, -1, keepdims=True)
    spread = jnp.mean(center * center, -1, keepdims=True)
    return center * lax.rsqrt(spread + epsilon) * gain + shift


def gelu_exact(value):
    return jax.nn.gelu(value, approximate=False)


def head_scores(query_blk, key_blk, owner, length):
    count = key_blk.shape[0]
    raw = jnp.einsum(
        "qhd,khd->hqk",
        query_blk.reshape(-1, HEADS, HEAD_DIM),
        key_blk.reshape(count, HEADS, HEAD_DIM),
        preferred_element_type=jnp.float32,
    )
    position = owner * count + jnp.arange(count, dtype=jnp.int32)
    return jnp.where((position < length)[None, None, :], raw * HEAD_DIM ** (-0.5), masked_score)


def block_grads(query_blk, grad_blk, log_blk, delta_blk, key_blk, value_blk, owner, length):
    rows = query_blk.shape[0]
    count = key_blk.shape[0]
    scores = head_scores(query_blk, key_blk, owner, length)
    probs = jnp.exp(scores - log_blk[:, :, None])
    probs_low = probs.astype(jnp.bfloat16)
    grad_heads = grad_blk.reshape(rows, HEADS, HEAD_DIM)
    query_heads = query_blk.reshape(rows, HEADS, HEAD_DIM)
    key_heads = key_blk.reshape(count, HEADS, HEAD_DIM)
    value_heads = value_blk.reshape(count, HEADS, HEAD_DIM)
    prob_grad = jnp.einsum(
        "qhd,khd->hqk", grad_heads, value_heads, preferred_element_type=jnp.float32
    )
    score_grad = (probs * (prob_grad - delta_blk[:, :, None])).astype(jnp.bfloat16)
    value_term = jnp.einsum(
        "hqk,qhd->khd", probs_low, grad_heads, preferred_element_type=jnp.float32
    )
    key_term = jnp.einsum(
        "hqk,qhd->khd", score_grad, query_heads, preferred_element_type=jnp.float32
    ) * HEAD_DIM ** (-0.5)
    query_term = jnp.einsum(
        "hqk,khd->qhd", score_grad, key_heads, preferred_element_type=jnp.float32
    ) * HEAD_DIM ** (-0.5)
    return (
        query_term.reshape(rows, -1),
        key_term.reshape(count, -1),
        value_term.reshape(count, -1),
    )


def body(
    tokens,
    lengths,
    w_query,
    b_query,
    w_key,
    w_value,
    b_value,
    w_out,
    b_out,
    gain_one,
    shift_one,
    w_up,
    b_up,
    w_down,
    b_down,
    gain_two,
    shift_two,
    cotangent,
):
    cycle = lax.axis_size("ctx")
    place = lax.axis_index("ctx")
    length = lengths[0]
    rows = tokens.shape[0]
    width = tokens.shape[1]
    gathered = (
        lax.all_gather(w_query, ("batch", "ctx"), axis=0, tiled=True),
        lax.all_gather(w_key, ("batch", "ctx"), axis=0, tiled=True),
        lax.all_gather(w_value, ("batch", "ctx"), axis=0, tiled=True),
        lax.all_gather(w_out, ("batch", "ctx"), axis=0, tiled=True),
        lax.all_gather(w_up, ("batch", "ctx"), axis=0, tiled=True),
        lax.all_gather(w_down, ("batch", "ctx"), axis=0, tiled=True),
        lax.all_gather(b_query, ("batch", "ctx"), axis=0, tiled=True),
        lax.all_gather(b_value, ("batch", "ctx"), axis=0, tiled=True),
        lax.all_gather(b_out, ("batch", "ctx"), axis=0, tiled=True),
        lax.all_gather(gain_one, ("batch", "ctx"), axis=0, tiled=True),
        lax.all_gather(shift_one, ("batch", "ctx"), axis=0, tiled=True),
        lax.all_gather(b_up, ("batch", "ctx"), axis=0, tiled=True),
        lax.all_gather(b_down, ("batch", "ctx"), axis=0, tiled=True),
        lax.all_gather(gain_two, ("batch", "ctx"), axis=0, tiled=True),
        lax.all_gather(shift_two, ("batch", "ctx"), axis=0, tiled=True),
    )
    query_full, key_full, value_full, out_full, up_full, down_full = gathered[:6]
    small = [item.astype(jnp.float32) for item in gathered[6:]]
    (
        bias_query,
        bias_value,
        bias_out,
        gain_first,
        shift_first,
        bias_up,
        bias_down,
        gain_second,
        shift_second,
    ) = small
    query_low = (
        jnp.dot(tokens, query_full, preferred_element_type=jnp.float32) + bias_query
    ).astype(jnp.bfloat16)
    key_low = jnp.dot(tokens, key_full, preferred_element_type=jnp.float32).astype(jnp.bfloat16)
    value_low = (
        jnp.dot(tokens, value_full, preferred_element_type=jnp.float32) + bias_value
    ).astype(jnp.bfloat16)
    start_top = jnp.full((HEADS, rows), masked_score, jnp.float32)
    start_total = jnp.zeros((HEADS, rows), jnp.float32)
    start_sum = jnp.zeros((rows, HEADS, HEAD_DIM), jnp.float32)

    def running(state, pair, owner):
        top, total, summed = state
        scores = head_scores(query_low, pair[0], owner, length)
        new_top = jnp.maximum(top, jnp.max(scores, -1))
        factor = jnp.exp(top - new_top)
        expos = jnp.exp(scores - new_top[:, :, None])
        total = total * factor + jnp.sum(expos, -1)
        summed = summed * factor.T[:, :, None] + jnp.einsum(
            "hqk,khd->qhd",
            expos.astype(jnp.bfloat16),
            pair[1].reshape(-1, HEADS, HEAD_DIM),
            preferred_element_type=jnp.float32,
        )
        return (new_top, total, summed)

    def run_step(step, carry):
        pair, state = carry
        state = running(state, pair, (place - step) % cycle)
        pair = shifted((pair[0], pair[1]), "ctx", 1)
        return (pair, state)

    pair, state = lax.fori_loop(
        0, cycle - 1, run_step, ((key_low, value_low), (start_top, start_total, start_sum))
    )
    top, total, summed = running(state, pair, (place + 1) % cycle)
    log_total = top + jnp.log(total)
    attended = (summed / total.T[:, :, None]).reshape(rows, width)
    mixed = attended.astype(jnp.bfloat16)
    projected = jnp.dot(mixed, out_full, preferred_element_type=jnp.float32) + bias_out
    first, first_back = jax.vjp(
        normalize, tokens.astype(jnp.float32) + projected, gain_first, shift_first
    )
    first_low = first.astype(jnp.bfloat16)
    inner = jnp.dot(first_low, up_full, preferred_element_type=jnp.float32) + bias_up
    active, gelu_back = jax.vjp(gelu_exact, inner)
    active_low = active.astype(jnp.bfloat16)
    branch = jnp.dot(active_low, down_full, preferred_element_type=jnp.float32) + bias_down
    result, second_back = jax.vjp(normalize, first + branch, gain_second, shift_second)
    output = result.astype(jnp.bfloat16)
    query_back, key_back, value_back, out_back, up_back, down_back = (
        query_full,
        key_full,
        value_full,
        out_full,
        up_full,
        down_full,
    )
    grad_second, grad_gain_two, grad_shift_two = second_back(cotangent.astype(jnp.float32))
    branch_grad = grad_second.astype(jnp.bfloat16)
    grad_b_down = jnp.sum(branch_grad.astype(jnp.float32), 0)
    grad_w_down = jnp.einsum(
        "tf,td->fd", active_low, branch_grad, preferred_element_type=jnp.float32
    )
    active_grad = jnp.einsum(
        "td,fd->tf", branch_grad, down_back, preferred_element_type=jnp.float32
    )
    inner_grad = gelu_back(active_grad)[0].astype(jnp.bfloat16)
    grad_b_up = jnp.sum(inner_grad.astype(jnp.float32), 0)
    grad_w_up = jnp.einsum("td,tf->df", first_low, inner_grad, preferred_element_type=jnp.float32)
    first_grad = (
        jnp.einsum("tf,df->td", inner_grad, up_back, preferred_element_type=jnp.float32)
        + grad_second
    )
    grad_first, grad_gain_one, grad_shift_one = first_back(first_grad)
    proj_grad = grad_first.astype(jnp.bfloat16)
    grad_b_out = jnp.sum(proj_grad.astype(jnp.float32), 0)
    grad_w_out = jnp.einsum("td,te->de", mixed, proj_grad, preferred_element_type=jnp.float32)
    mixed_grad = jnp.einsum(
        "te,de->td", proj_grad, out_back, preferred_element_type=jnp.float32
    ).astype(jnp.bfloat16)
    delta = jnp.sum(
        (mixed_grad.astype(jnp.float32) * attended).reshape(rows, HEADS, HEAD_DIM), -1
    ).T
    zeros = jnp.zeros((rows, width), jnp.float32)

    def move_key_grads(grads):
        return (
            shifted(grads[0].astype(jnp.bfloat16), "ctx", 1).astype(jnp.float32),
            shifted(grads[1].astype(jnp.bfloat16), "ctx", 1).astype(jnp.float32),
        )

    def key_step(step, carry):
        blocks, grads, query_acc = carry
        query_term, key_term, value_term = block_grads(
            query_low,
            mixed_grad,
            log_total,
            delta,
            blocks[0],
            blocks[1],
            (place - step) % cycle,
            length,
        )
        grads = move_key_grads((grads[0] + key_term, grads[1] + value_term))
        blocks = shifted((blocks[0], blocks[1]), "ctx", 1)
        return (blocks, grads, query_acc + query_term)

    blocks, grads, query_acc = lax.fori_loop(
        0, cycle - 1, key_step, ((key_low, value_low), (zeros, zeros), zeros)
    )
    query_term, key_term, value_term = block_grads(
        query_low, mixed_grad, log_total, delta, blocks[0], blocks[1], (place + 1) % cycle, length
    )
    key_acc, value_acc = move_key_grads((grads[0] + key_term, grads[1] + value_term))
    query_acc = query_acc + query_term
    query_grad = query_acc.astype(jnp.bfloat16)
    key_grad = key_acc.astype(jnp.bfloat16)
    value_grad = value_acc.astype(jnp.bfloat16)
    grad_b_query = jnp.sum(query_grad.astype(jnp.float32), 0)
    grad_b_value = jnp.sum(value_grad.astype(jnp.float32), 0)
    grad_w_query = jnp.einsum("td,te->de", tokens, query_grad, preferred_element_type=jnp.float32)
    grad_w_key = jnp.einsum("td,te->de", tokens, key_grad, preferred_element_type=jnp.float32)
    grad_w_value = jnp.einsum("td,te->de", tokens, value_grad, preferred_element_type=jnp.float32)
    token_grad = grad_first + jnp.einsum(
        "te,de->td", query_grad, query_back, preferred_element_type=jnp.float32
    )
    token_grad = token_grad + jnp.einsum(
        "te,de->td", key_grad, key_back, preferred_element_type=jnp.float32
    )
    token_grad = token_grad + jnp.einsum(
        "te,de->td", value_grad, value_back, preferred_element_type=jnp.float32
    )
    grad_tokens = token_grad.astype(jnp.bfloat16)
    sharded = (
        lax.psum_scatter(grad_w_query, ("batch", "ctx"), scatter_dimension=0, tiled=True),
        lax.psum_scatter(grad_b_query, ("batch", "ctx"), scatter_dimension=0, tiled=True),
        lax.psum_scatter(grad_w_key, ("batch", "ctx"), scatter_dimension=0, tiled=True),
        lax.psum_scatter(grad_w_value, ("batch", "ctx"), scatter_dimension=0, tiled=True),
        lax.psum_scatter(grad_b_value, ("batch", "ctx"), scatter_dimension=0, tiled=True),
        lax.psum_scatter(grad_w_out, ("batch", "ctx"), scatter_dimension=0, tiled=True),
        lax.psum_scatter(grad_b_out, ("batch", "ctx"), scatter_dimension=0, tiled=True),
        lax.psum_scatter(grad_gain_one, ("batch", "ctx"), scatter_dimension=0, tiled=True),
        lax.psum_scatter(grad_shift_one, ("batch", "ctx"), scatter_dimension=0, tiled=True),
        lax.psum_scatter(grad_w_up, ("batch", "ctx"), scatter_dimension=0, tiled=True),
        lax.psum_scatter(grad_b_up, ("batch", "ctx"), scatter_dimension=0, tiled=True),
        lax.psum_scatter(grad_w_down, ("batch", "ctx"), scatter_dimension=0, tiled=True),
        lax.psum_scatter(grad_b_down, ("batch", "ctx"), scatter_dimension=0, tiled=True),
        lax.psum_scatter(grad_gain_two, ("batch", "ctx"), scatter_dimension=0, tiled=True),
        lax.psum_scatter(grad_shift_two, ("batch", "ctx"), scatter_dimension=0, tiled=True),
    )
    return (
        output,
        grad_tokens,
        sharded[0],
        sharded[1],
        sharded[2],
        sharded[3],
        sharded[4],
        sharded[5],
        sharded[6],
        sharded[7],
        sharded[8],
        sharded[9],
        sharded[10],
        sharded[11],
        sharded[12],
        sharded[13],
        sharded[14],
    )


def normal_parts(resid):
    center = resid - jnp.mean(resid, -1, keepdims=True)
    spread = jnp.mean(center * center, -1, keepdims=True)
    scale = lax.rsqrt(spread + epsilon)
    return center * scale, scale


def normal_back(hat, scale, grad):
    inner = jnp.mean(grad * hat, -1, keepdims=True)
    return scale * (grad - jnp.mean(grad, -1, keepdims=True) - hat * inner)


def dot(left, right, dims=((1,), (0,))):
    return lax.dot_general(left, right, (dims, ((), ())), preferred_element_type=jnp.float32)


def head_rows(block, head, extra):
    row = lax.broadcasted_iota(jnp.int32, block.shape, 0)
    keep = (row >= head * HEAD_DIM) & (row < (head + 1) * HEAD_DIM)
    if extra:
        keep = keep | (row >= extra)
    return jnp.where(keep, block, jnp.zeros_like(block))


def head_lanes(block, head):
    lane = lax.broadcasted_iota(jnp.int32, block.shape, 1)
    keep = (lane >= head * HEAD_DIM) & (lane < (head + 1) * HEAD_DIM)
    return jnp.where(keep, block, jnp.zeros_like(block))


def copied_kernel(kernel, first, far, count, shapes, *refs):
    operands, refs = refs[:count], refs[count:]
    results, refs = refs[: len(shapes)], refs[len(shapes) :]
    moved = [i for i in range(count) if i >= first and i not in far]
    taken, refs = refs[: len(moved)], refs[len(moved) :]
    given, refs = refs[: len(shapes)], refs[len(shapes) :]
    coming, going, rest = refs[0], refs[1], refs[2:]
    local = list(operands)
    copies = []
    for index, at in enumerate(moved):
        copies.append(pltpu.make_async_copy(operands[at], taken[index], coming.at[index]))
        local[at] = taken[index]
    for copy in copies:
        copy.start()
    for copy in copies:
        copy.wait()
    copies = [
        pltpu.make_async_copy(given[index], results[index], going.at[index])
        for index in range(len(shapes))
    ]
    kernel(*local, *given, *rest, leave=lambda *which: [copies[index].start() for index in which])
    for copy in copies:
        copy.wait()


def one_step(
    kernel, operands, shapes, flops, name, first=1, far=(), scratch=(), exps=0, limit=14
):
    specs = []
    for index in range(len(operands)):
        if index < first:
            specs.append(pl.BlockSpec(memory_space=pltpu.SMEM))
        elif index in far:
            specs.append(pl.BlockSpec(memory_space=pl.ANY))
        else:
            specs.append(pl.BlockSpec(memory_space=pltpu.HBM))
    moved = [
        pltpu.VMEM(operand.shape, operand.dtype)
        for index, operand in enumerate(operands)
        if index >= first and index not in far
    ]
    given = [pltpu.VMEM(*shape) for shape in shapes]
    return pl.pallas_call(
        functools.partial(copied_kernel, kernel, first, far, len(operands), shapes),
        in_specs=specs,
        out_specs=[pl.BlockSpec(memory_space=pltpu.HBM)] * len(shapes),
        out_shape=[pltpu.HBM(*shape) for shape in shapes],
        scratch_shapes=moved
        + given
        + [pltpu.SemaphoreType.DMA((len(moved),)), pltpu.SemaphoreType.DMA((len(shapes),))]
        + list(scratch),
        compiler_params=pltpu.CompilerParams(vmem_limit_bytes=limit * 2**20),
        cost_estimate=pl.CostEstimate(
            flops=flops,
            bytes_accessed=sum(operand.size * operand.dtype.itemsize for operand in operands),
            transcendentals=exps,
        ),
        name=name,
    )(*operands)


def turn(block):
    return jnp.transpose(block.astype(jnp.float32)).astype(block.dtype)


def attend_kernel(heads, chips, places, *refs, leave):
    own, others = refs[:chips], refs[chips : 2 * chips]
    weight, bias_query, bias_value = refs[2 * chips : 2 * chips + 3]
    refs = refs[2 * chips + 3 :]
    mine_ref, query, key, value, att, log = refs[:6]
    sent, (every, query_t, value_t, mixed) = refs[6 : 6 + chips], refs[6 + chips :]
    low, f32 = jnp.bfloat16, jnp.float32
    width = heads * HEAD_DIM
    count, rows, depth = every.shape
    spare = key.shape[1] - width

    for distance in range(chips):
        slot = lax.rem(places[0] - distance + chips, chips)
        every[slot] = own[distance][:rows, :]
        every[chips + slot] = others[distance][:rows, :]
    tokens = every[...].reshape(count * rows, depth)
    mine = chips * rows
    mine_ref[...] = tokens[:mine]
    first = dot(tokens[:mine], weight[:, :width]) + bias_query[...]
    first = (first.astype(low).astype(f32) * HEAD_DIM ** (-0.5)).astype(low)
    query[...] = first
    one = lax.broadcasted_iota(jnp.int32, (spare, mine), 0) == 0
    query_t[...] = jnp.concatenate([turn(first), jnp.where(one, 1.0, 0.0).astype(low)], 0)
    second = dot(tokens, weight[:, width : 2 * width]).astype(low)
    row = lax.broadcasted_iota(jnp.int32, (rows, spare), 0)
    lane = lax.broadcasted_iota(jnp.int32, (rows, spare), 1)
    for block in range(count):
        hide = jnp.where((row < places[1 + block]) | (lane > 0), 0.0, masked_score)
        at = slice(block * rows, (block + 1) * rows)
        key[at, :] = jnp.concatenate([second[at].astype(f32), hide], 1).astype(low)
    third = (dot(tokens, weight[:, 2 * width :]) + bias_value[...]).astype(low)
    value[...] = third
    value_t[...] = turn(third)
    leave(0, 1, 2, 3)

    pieces = 2 if chips % 2 == 0 else 1
    for step in range(chips // pieces):
        span = slice(step * pieces * rows, (step + 1) * pieces * rows)
        for head in range(heads):
            scores = dot(key[...], head_rows(query_t[:, span], head, width))
            top = jnp.max(scores, 0, keepdims=True)
            expos = jnp.exp(scores - top)
            total = jnp.sum(expos, 0, keepdims=True)
            at = slice(head * HEAD_DIM, (head + 1) * HEAD_DIM)
            summed = dot(value_t[at, :], expos.astype(low)) / total
            att[at, span] = summed
            for piece in range(pieces):
                mixed[step * pieces + piece, at, :] = summed[
                    :, piece * rows : (piece + 1) * rows
                ].astype(low)
            log[head : head + 1, span] = top + jnp.log(total)
    for distance in range(chips):
        sent[distance][...] = mixed[lax.rem(places[0] + distance, chips)]
    leave(*range(4, 6 + chips))


def attend(heads, places, own, others, weight, bias_query, bias_value):
    chips = len(own)
    rows, depth = own[0].shape
    count = 2 * chips
    mine, keys = chips * rows, count * rows
    width = heads * HEAD_DIM
    wide = -(-(width + 1) // 128) * 128
    low, f32 = jnp.bfloat16, jnp.float32
    return one_step(
        functools.partial(attend_kernel, heads, chips),
        [places, *own, *others, weight, bias_query, bias_value],
        [
            ((mine, depth), low),
            ((mine, width), low),
            ((keys, wide), low),
            ((keys, width), low),
            ((width, mine), f32),
            ((heads, mine), f32),
        ]
        + [((width, rows), low)] * chips,
        flops=4 * heads * mine * keys * 256 + 6 * keys * depth * width,
        name="attend",
        scratch=[
            pltpu.VMEM((count, rows, depth), low),
            pltpu.VMEM((wide, mine), low),
            pltpu.VMEM((width, keys), low),
            pltpu.VMEM((chips, width, rows), low),
        ],
        exps=heads * mine * keys,
    )


def attend_back_kernel(heads, chips, places, query, key, value, att, log, *refs, leave):
    come_refs, refs = refs[:chips], refs[chips + 1 :]
    query_grad, kept, away, key_sum, value_sum, grad_t, query_t, key_t = refs
    low = jnp.bfloat16
    width, rows = come_refs[0].shape
    mine = chips * rows
    for distance in range(chips):
        slot = lax.rem(places[0] - distance + chips, chips)
        grad_t[slot] = come_refs[distance][...]
    one = lax.broadcasted_iota(jnp.int32, (key.shape[1] - width, mine), 0) == 0
    query_t[...] = jnp.concatenate([turn(query[...]), jnp.where(one, 1.0, 0.0).astype(low)], 0)
    key_t[...] = turn(key[:, :width])
    pieces = 2 if chips % 2 == 0 else 1
    for step in range(chips // pieces):
        span = slice(step * pieces * rows, (step + 1) * pieces * rows)
        come = jnp.concatenate([grad_t[step * pieces + piece] for piece in range(pieces)], 1)
        come_rows = turn(come)
        turned = []
        for head in range(heads):
            at = slice(head * HEAD_DIM, (head + 1) * HEAD_DIM)
            scores = dot(key[...], head_rows(query_t[:, span], head, width))
            probs = jnp.exp(scores - log[head : head + 1, span])
            prob_grad = dot(value[...], head_rows(come, head, 0))
            delta = jnp.sum(come[at].astype(jnp.float32) * att[at, span], 0, keepdims=True)
            score_grad = (probs * (prob_grad - delta)).astype(low)
            turned.append(dot(key_t[at, :], score_grad))
            key_term = dot(score_grad, head_lanes(query[span, :], head))
            value_term = dot(probs.astype(low), head_lanes(come_rows, head))
            if step == 0 and head == 0:
                key_sum[...] = key_term
                value_sum[...] = value_term
            else:
                key_sum[...] += key_term
                value_sum[...] += value_term
        gathered = jnp.concatenate(turned, 0) * HEAD_DIM ** (-0.5)
        query_grad[span, :] = jnp.transpose(gathered).astype(low)
    kept[...] = jnp.concatenate([key_sum[:mine, :], value_sum[:mine, :]], 1)
    away[...] = jnp.concatenate([key_sum[mine:, :], value_sum[mine:, :]], 1).astype(low)
    leave(0, 1, 2)


def attend_back(heads, places, query, key, value, att, log, come, marker):
    chips = len(come)
    mine, width = query.shape
    keys, wide = key.shape
    low, f32 = jnp.bfloat16, jnp.float32
    return one_step(
        functools.partial(attend_back_kernel, heads, chips),
        [places, query, key, value, att, log, *come, marker],
        [((mine, width), low), ((mine, 2 * width), f32), ((keys - mine, 2 * width), low)],
        flops=10 * heads * mine * keys * 256,
        name="attend_back",
        far=(6 + chips,),
        scratch=[
            pltpu.VMEM((keys, width), f32),
            pltpu.VMEM((keys, width), f32),
            pltpu.VMEM((chips, width, mine // chips), low),
            pltpu.VMEM((wide, mine), low),
            pltpu.VMEM((width, keys), low),
        ],
        exps=heads * mine * keys,
    )


def finish_kernel(
    places, mine, weight, query_grad, kept, come, short, marker, *refs, leave
):
    low, f32 = jnp.bfloat16, jnp.float32
    token_part, own_terms, away_terms, terms = refs
    owners, _, part, width = terms.shape
    pair = (kept[...] + come[...].astype(f32)).astype(low)
    grads = jnp.concatenate([query_grad[...].astype(f32), pair.astype(f32)], 1)
    sums = jnp.sum(grads, 0, keepdims=True)
    grads = grads.astype(low)
    part_grad = dot(grads, weight[...], ((1,), (1,))).astype(low)
    token_part[...] = part_grad.reshape(token_part.shape)
    leave(0)
    terms[...] = dot(mine[...], grads, ((0,), (0,))).reshape(terms.shape)
    core = places[1]
    count = short.shape[2]
    row = lax.broadcasted_iota(jnp.int32, (count, width), 0)
    below = jnp.where(row == count - 1, sums, 0.0)
    for index, ref, which in ((1, away_terms, 1 - core), (0, own_terms, core)):
        for owner in range(owners):
            block = [terms[owner, which], short[owner, which] + below]
            ref[owner] = jnp.concatenate(block, 0).astype(ref.dtype)
        leave(1 + index)


def finish(chips, places, mine, weight, query_grad, kept, come, short, marker):
    count, depth = mine.shape
    width = weight.shape[1]
    owners = short.shape[0]
    part = depth // (2 * owners)
    held = part + short.shape[2]
    return one_step(
        finish_kernel,
        [places, mine, weight, query_grad, kept, come, short, marker],
        [
            ((chips, count // chips, depth), jnp.bfloat16),
            ((owners, held, width), jnp.float32),
            ((owners, held, width), jnp.bfloat16),
        ],
        flops=4 * count * depth * width,
        name="finish",
        far=(7,),
        scratch=[pltpu.VMEM((owners, 2, part, width), jnp.float32)],
    )


def bundle_kernel(places, own, come, w_up, *outs, leave):
    f32 = jnp.float32
    teams, part, width = w_up.shape
    owners, held, group = own.shape
    chips = owners // teams
    for distance, out in enumerate(outs):
        team = lax.rem(places[0] + distance, teams)
        for chip in range(chips):
            owner = team * chips + chip
            block = own[owner] + come[owner].astype(f32)
            block = jnp.pad(block, ((0, 0), (0, width - group)))
            out[chip * held : (chip + 1) * held] = block.astype(out.dtype)
        out[chips * held :] = w_up[team]
        leave(distance)


def bundle(places, own, come, w_up):
    teams, part, width = w_up.shape
    owners, held, _ = own.shape
    shape = (owners // teams * held + part, width)
    return one_step(
        bundle_kernel,
        [places, own, come, w_up],
        [(shape, jnp.bfloat16)] * teams,
        flops=0,
        limit=8,
        name="bundle",
    )


def unpack_kernel(part, group, found, *outs, leave):
    chips, count, _ = found.shape
    blocks = [found[chip].astype(jnp.float32) for chip in range(chips)]
    for index in range(3):
        columns = slice(index * group, (index + 1) * group)
        outs[index][...] = jnp.concatenate([block[:part, columns] for block in blocks], 1)
    total = blocks[0]
    for block in blocks[1:]:
        total = total + block
    outs[3][...] = total[count - part :]
    outs[4][...] = total[part : count - part]
    outs[5][...] = jnp.concatenate([b[count - part - 1 : count - part] for b in blocks], 0)
    leave(*range(6))


def unpack(part, group, found):
    chips, count, width = found.shape
    shapes = [((part, width), jnp.float32)] * 4
    shapes.append(((count - 2 * part, width), jnp.float32))
    shapes.append(((chips, width), jnp.float32))
    return one_step(
        functools.partial(unpack_kernel, part, group),
        [found],
        shapes,
        flops=found.size,
        limit=8,
        name="unpack",
        first=0,
    )


def wait_kernel(*refs):
    pass


def after(block, *others, pinned=False):
    anywhere = pl.BlockSpec(memory_space=pl.ANY)
    shape = jax.ShapeDtypeStruct(block.shape, block.dtype)
    if pinned:
        block = pltpu.with_memory_space_constraint(block, pltpu.HBM)
        shape = pltpu.HBM(block.shape, block.dtype)
    return pl.pallas_call(
        wait_kernel,
        in_specs=[anywhere] * (1 + len(others)),
        out_specs=anywhere,
        out_shape=shape,
        input_output_aliases={0: 0},
        compiler_params=pltpu.CompilerParams(vmem_limit_bytes=2**20),
        name="after",
    )(block, *others)


def lay_kernel(tokens, w_out, both):
    both[...] = jnp.concatenate([tokens[...], w_out[...]], 0)


def lay(tokens, w_out):
    shape = (tokens.shape[0] + w_out.shape[0], tokens.shape[1])
    return pl.pallas_call(
        lay_kernel,
        in_specs=[pl.BlockSpec(memory_space=pltpu.VMEM)] * 2,
        out_specs=pl.BlockSpec(memory_space=pltpu.VMEM),
        out_shape=jax.ShapeDtypeStruct(shape, tokens.dtype),
        name="lay",
    )(tokens, w_out)


def pack_kernel(chips, w_query, w_key, w_value, vectors, b_up, out):
    part = w_query.shape[0]
    group = w_query.shape[1] // chips
    count = vectors.shape[0]
    rest = out.shape[1] - part
    short = jnp.concatenate(
        [
            jnp.pad(vectors[...].astype(jnp.float32), ((0, rest - count), (0, 128 - part))),
            jnp.pad(
                b_up[...].astype(jnp.float32),
                ((0, rest - 1), (0, 3 * group - 128 - b_up.shape[1])),
            ),
        ],
        1,
    )
    for index in range(chips):
        columns = slice(index * group, (index + 1) * group)
        block = jnp.concatenate(
            [item[:, columns].astype(jnp.float32) for item in (w_query, w_key, w_value)], 1
        )
        both = jnp.concatenate([block, short], 0)
        spare = out.shape[2] - both.shape[1]
        out[index] = jnp.pad(both, ((0, 0), (0, spare))).astype(jnp.bfloat16)


def pack(chips, w_query, w_key, w_value, vectors, b_up, held):
    part, width = w_query.shape
    return pl.pallas_call(
        functools.partial(pack_kernel, chips),
        in_specs=[pl.BlockSpec(memory_space=pltpu.VMEM)] * 5,
        out_specs=pl.BlockSpec(memory_space=pltpu.VMEM),
        out_shape=jax.ShapeDtypeStruct((chips, held, width), jnp.bfloat16),
        name="pack",
    )(w_query, w_key, w_value, vectors, b_up)


def share_kernel(packed, w_up, out):
    teams, count, width = out.shape
    chips, held, _ = packed.shape
    for team in range(teams):
        for chip in range(chips):
            out[team, chip * held : (chip + 1) * held] = packed[chip]
        out[team, chips * held :] = w_up[:, team * width : (team + 1) * width]


def share(teams, packed, w_up):
    chips, held, width = packed.shape
    part, hidden = w_up.shape
    return pl.pallas_call(
        share_kernel,
        in_specs=[pl.BlockSpec(memory_space=pltpu.VMEM)] * 2,
        out_specs=pl.BlockSpec(memory_space=pltpu.VMEM),
        out_shape=jax.ShapeDtypeStruct(
            (teams, chips * held + part, hidden // teams), jnp.bfloat16
        ),
        name="share",
    )(packed, w_up)


def pick(blocks, index, axis=0):
    return lax.dynamic_index_in_dim(blocks, index, axis, keepdims=False)


def ordered(found, me):
    count = len(found)
    rising = [found[count - 1 - i] for i in range(count)]
    twice = jnp.stack(rising + rising[:-1], 0)
    return lax.dynamic_slice_in_dim(twice, count - 1 - me, count, 0)


def layer_split(
    tokens,
    lengths,
    w_query,
    b_query,
    w_key,
    w_value,
    b_value,
    w_out,
    b_out,
    gain_one,
    shift_one,
    w_up,
    b_up,
    w_down,
    b_down,
    gain_two,
    shift_two,
    cotangent,
):
    f32, low = jnp.float32, jnp.bfloat16
    teams = lax.axis_size("batch")
    chips = lax.axis_size("ctx") // 2
    team = lax.axis_index("batch")
    place = lax.axis_index("ctx")
    chip, core = place // 2, place % 2
    rows, width = tokens.shape
    part = w_query.shape[0]
    hidden = w_up.shape[1]
    quarter = hidden // teams
    heads = HEADS // chips
    group = heads * HEAD_DIM
    length = lengths[0]

    def to_chip(block, distance):
        route = [(i, (i // 2 + distance) % chips * 2 + i % 2) for i in range(2 * chips)]
        return lax.ppermute(block, "ctx", route)

    def to_core(block):
        return lax.ppermute(block, "ctx", [(i, i ^ 1) for i in range(2 * chips)])

    def to_team(block, distance):
        return lax.ppermute(block, "batch", [(i, (i + distance) % teams) for i in range(teams)])

    def from_chips(block):
        return [block] + [to_chip(block, d) for d in range(1, chips)]

    def from_teams(block):
        return [block] + [to_team(block, d) for d in range(1, teams)]

    def swap_chips(blocks, axis=0):
        return [pick(blocks, chip, axis)] + [
            to_chip(pick(blocks, (chip + d) % chips, axis), d) for d in range(1, chips)
        ]

    def swap_teams(blocks, axis=0):
        return [pick(blocks, team, axis)] + [
            to_team(pick(blocks, (team + d) % teams, axis), d) for d in range(1, teams)
        ]

    same_core = [[2 * z + c for z in range(chips)] for c in range(2)]

    def trade_chips(blocks):
        return lax.all_to_all(blocks, "ctx", 0, 0, axis_index_groups=same_core)

    def trade_teams(blocks):
        return lax.all_to_all(blocks, "batch", 0, 0)

    def both_cores(block, axis):
        other = to_core(block)
        first = jnp.where(core == 0, block, other)
        second = jnp.where(core == 0, other, block)
        return jnp.stack([first, second], axis)

    def cores_sum(terms, axis):
        away = to_core(pick(terms, 1 - core, axis).astype(low))
        return pick(terms, core, axis).astype(f32) + away.astype(f32)

    def total(blocks):
        result = blocks[0].astype(f32)
        for block in blocks[1:]:
            result = result + block.astype(f32)
        return result

    def return_teams(blocks):
        return total(
            [blocks[0]] + [to_team(blocks[d].astype(low), -d) for d in range(1, teams)]
        )

    vectors = (
        b_query,
        b_value,
        b_out,
        gain_one,
        shift_one,
        b_down,
        gain_two,
        shift_two,
    )
    held = -(-(part + len(vectors)) // 16) * 16
    laid = lay(tokens, w_out)
    packed = pack(
        chips,
        w_query,
        w_key,
        w_value,
        jnp.stack(vectors),
        b_up[None],
        held,
    )
    packed = trade_chips(packed)
    pieces = from_chips(after(laid, packed, pinned=True))
    traded = trade_teams(share(teams, packed, w_up))
    up_blocks = traded[:, chips * held :]
    packed = both_cores(traded[:, : chips * held].reshape(teams, chips, held, width), 2)
    w_heads = packed[:, :, :, :part, : 3 * group].reshape(width, 3 * group)
    shorts = packed[:, :, :, part:].reshape(teams * chips * 2, held - part, width)

    rows_of = shorts[:, :, :part].transpose(1, 0, 2).reshape(held - part, width)
    bias_query, bias_value, bias_out, gain_first, shift_first = rows_of[:5].astype(f32)
    bias_down, gain_second, shift_second = rows_of[5:8].astype(f32)
    bias_up = shorts[:, 0, 128 : 128 + b_up.shape[0]].reshape(-1).astype(f32)
    bias_up = lax.dynamic_slice_in_dim(bias_up, team * quarter, quarter)
    bias_query = lax.dynamic_slice_in_dim(bias_query, chip * group, group)
    bias_value = lax.dynamic_slice_in_dim(bias_value, chip * group, group)

    others = [to_core(tokens)] + [to_core(piece) for piece in pieces[1:]]
    starts = jnp.arange(chips, dtype=jnp.int32) * (2 * rows)
    starts = jnp.concatenate([starts + core * rows, starts + (1 - core) * rows])
    places = jnp.concatenate([chip[None], length - starts])

    out_rel = [w_out] + [piece[rows:] for piece in pieces[1:]]
    later = jnp.concatenate([up_blocks.reshape(teams * part, quarter), w_down], 0)
    later = lax.all_gather(later, "ctx", axis=0)
    out_blocks = after(ordered(out_rel, chip), w_heads)
    out_blocks = trade_teams(jnp.broadcast_to(out_blocks[None], (teams,) + out_blocks.shape))

    mine, query, key, value, attended, log_total, *mixed_out = attend(
        heads,
        places,
        [tokens] + pieces[1:],
        others,
        w_heads,
        bias_query[None],
        bias_value[None],
    )
    up_part = later[:, : teams * part].reshape(2 * chips, teams, part, quarter)
    up_part = up_part.transpose(1, 0, 2, 3).reshape(width, quarter)
    down_part = later[:, teams * part :].reshape(quarter, width)
    out_full = both_cores(after(out_blocks, log_total), 2).reshape(width, width)

    tn = ((0,), (0,))
    mixed_rel = [mixed_out[0]] + [to_chip(mixed_out[d], d) for d in range(1, chips)]
    mixed_t = ordered(mixed_rel, chip).reshape(width, rows)
    projected = dot(mixed_t, out_full, tn) + bias_out
    hat_one, scale_one = normal_parts(tokens.astype(f32) + projected)
    first = hat_one * gain_first + shift_first
    first_low = first.astype(low)

    wide = jnp.concatenate(from_teams(first_low), 0)
    inner = dot(wide, up_part) + bias_up
    cdf = 0.5 * (1.0 + lax.erf(inner * 2.0**-0.5))
    slope = cdf + inner * (jnp.exp(-0.5 * inner * inner) * (2.0 * math.pi) ** -0.5)
    active_low = (inner * cdf).astype(low)
    active_low, slope = lax.optimization_barrier((active_low, slope))
    branch_part = dot(active_low, down_part)
    branch = return_teams(branch_part.reshape(teams, rows, width)) + bias_down
    hat_two, scale_two = normal_parts(first + branch)
    output = (hat_two * gain_second + shift_second).astype(low)
    grad_out = cotangent.astype(f32)
    grad_gain_two = jnp.sum(grad_out * hat_two, 0)
    grad_shift_two = jnp.sum(grad_out, 0)
    grad_second = normal_back(hat_two, scale_two, grad_out * gain_second)
    branch_grad = grad_second.astype(low)
    grad_b_down = jnp.sum(branch_grad.astype(f32), 0)
    wide_grad = jnp.concatenate(from_teams(branch_grad), 0)
    active_grad = dot(wide_grad, down_part, ((1,), (1,)))
    inner_grad = (active_grad * slope).astype(low)
    first_part = dot(inner_grad, up_part, ((1,), (1,))).astype(low)
    first_part = first_part.reshape(teams, rows, width)
    leaving = [first_part[d] for d in range(teams)]
    come_back = [to_team(leaving[d], -d) for d in range(1, teams)]
    first_grad = total([leaving[0]] + come_back) + grad_second
    grad_b_up = jnp.sum(inner_grad.astype(f32), 0)
    grad_down = dot(active_low, after(wide_grad, leaving[1]), tn)
    grad_up = dot(wide, after(inner_grad, leaving[1]), tn)

    grad_gain_one = jnp.sum(first_grad * hat_one, 0)
    grad_shift_one = jnp.sum(first_grad, 0)
    grad_first = normal_back(hat_one, scale_one, first_grad * gain_first)
    proj_grad = grad_first.astype(low)
    grad_b_out = jnp.sum(proj_grad.astype(f32), 0)
    mixed_grad_t = dot(out_full, proj_grad, ((1,), (1,))).astype(low)
    mixed_grad_t = mixed_grad_t.reshape(chips, group, rows)
    leaving = [pick(mixed_grad_t, (chip + d) % chips) for d in range(chips)]
    grad_out_w = dot(mixed_t, after(proj_grad, leaving[1]))
    out_sum = cores_sum(grad_out_w.reshape(teams, chips, 2, part, width), 2).astype(low)

    come = [leaving[0]] + [to_chip(leaving[d], d) for d in range(1, chips)]
    query_grad, kept, away = attend_back(
        heads, places, query, key, value, attended, log_total, come, out_sum
    )
    up_terms = grad_up.astype(low).reshape(teams, 2 * chips, part, quarter)
    up_terms = up_terms.transpose(1, 0, 2, 3).reshape(2 * chips, teams * part, quarter)
    down_terms = grad_down.astype(low).reshape(2 * chips, -1, width)
    sums = lax.psum_scatter(
        jnp.concatenate([up_terms, down_terms], 1), "ctx", scatter_dimension=0, tiled=False
    )
    up_sum = sums[: teams * part].reshape(teams, part, quarter)

    out_traded = trade_teams(out_sum)
    small = (
        grad_b_out,
        grad_gain_one,
        grad_shift_one,
        grad_b_down,
        grad_gain_two,
        grad_shift_two,
    )
    small = jnp.stack([item.reshape(teams * chips, 2, part) for item in small], 2)
    small = jnp.pad(small, ((0, 0),) * 2 + ((0, held - part - len(vectors) + 2), (0, 128 - part)))
    tall = lax.dynamic_update_slice_in_dim(
        jnp.zeros((hidden,), f32), grad_b_up, team * quarter, 0
    ).reshape(teams * chips, 2, 1, -1)
    lanes = 3 * group - 128 - tall.shape[-1]
    tall = jnp.pad(tall, ((0, 0),) * 2 + ((0, held - part - 1), (0, lanes)))
    token_part, own_terms, away_terms = finish(
        chips,
        jnp.stack([chip, core]),
        mine,
        w_heads,
        query_grad,
        kept,
        to_core(away),
        jnp.concatenate([small, tall], 3),
        out_traded,
    )
    bundles = bundle(team[None], own_terms, to_core(away_terms), up_sum)
    traded = [bundles[0]] + [to_team(bundles[d], d) for d in range(1, teams)]
    token_come = trade_chips(token_part)
    token_come = after(token_come, *traded[1:])
    token_grad = grad_first + jnp.sum(token_come.astype(f32), 0)
    grad_tokens = token_grad.astype(low)
    out_up = ordered([block[-part:] for block in traded], team)
    out_up = out_up.transpose(1, 0, 2).reshape(part, hidden).astype(f32)
    terms = total([block[:-part] for block in traded]).astype(low)
    out_down = after(sums, traded[1])[teams * part :].astype(f32)
    out_sum = jnp.sum(out_traded.astype(f32), 0).astype(low)
    terms = jnp.concatenate([terms.reshape(chips, held, width), out_sum], 1)
    found = trade_chips(after(terms, grad_tokens))
    out_query, out_key, out_value, out_out, short_sum, sums = unpack(part, group, found)
    vec = [short_sum[i, :part] for i in range(6)]
    out_b_up = short_sum[0, 128 : 128 + b_up.shape[0]]
    own_sums = lax.dynamic_slice(sums, (team, 0), (1, 3 * group))[0].reshape(3, group)
    own_sums = lax.dynamic_slice(own_sums, (0, place * part), (3, part))
    return (
        output,
        grad_tokens,
        out_query,
        own_sums[0],
        out_key,
        out_value,
        own_sums[2],
        out_out,
        vec[0],
        vec[1],
        vec[2],
        out_up,
        out_b_up,
        out_down,
        vec[3],
        vec[4],
        vec[5],
    )


def solution(mesh):
    in_specs = (
        P(("batch", "ctx"), None),
        P("batch"),
        P(("batch", "ctx"), None),
        P(("batch", "ctx")),
        P(("batch", "ctx"), None),
        P(("batch", "ctx"), None),
        P(("batch", "ctx")),
        P(("batch", "ctx"), None),
        P(("batch", "ctx")),
        P(("batch", "ctx")),
        P(("batch", "ctx")),
        P(("batch", "ctx"), None),
        P(("batch", "ctx")),
        P(("batch", "ctx"), None),
        P(("batch", "ctx")),
        P(("batch", "ctx")),
        P(("batch", "ctx")),
        P(("batch", "ctx"), None),
    )
    out_specs = (
        P(("batch", "ctx"), None),
        P(("batch", "ctx"), None),
        P(("batch", "ctx"), None),
        P(("batch", "ctx")),
        P(("batch", "ctx"), None),
        P(("batch", "ctx"), None),
        P(("batch", "ctx")),
        P(("batch", "ctx"), None),
        P(("batch", "ctx")),
        P(("batch", "ctx")),
        P(("batch", "ctx")),
        P(("batch", "ctx"), None),
        P(("batch", "ctx")),
        P(("batch", "ctx"), None),
        P(("batch", "ctx")),
        P(("batch", "ctx")),
        P(("batch", "ctx")),
    )
    places = mesh.shape["ctx"]
    whole_heads = places % 2 == 0 and HEADS % (places // 2) == 0
    step = layer_split if whole_heads else body
    return jax.shard_map(step, mesh=mesh, in_specs=in_specs, out_specs=out_specs, check_vma=False)
```

```python
import functools
import math

import jax
import jax.numpy as jnp
from jax import lax
from jax.experimental import pallas as pl
from jax.experimental.pallas import tpu as pltpu
from jax.sharding import PartitionSpec as P

HEADS = 12
HEAD_DIM = 64


epsilon = 1e-06
masked_score = -1e30


def shifted(block, axis, distance):
    devices = range(lax.axis_size(axis))
    route = [((i - distance) % len(devices), i) for i in devices]
    return lax.ppermute(block, axis, route)


def normalize(resid, gain, shift):
    center = resid - jnp.mean(resid, -1, keepdims=True)
    spread = jnp.mean(center * center, -1, keepdims=True)
    return center * lax.rsqrt(spread + epsilon) * gain + shift


def gelu_exact(value):
    return jax.nn.gelu(value, approximate=False)


def head_scores(query_blk, key_blk, owner, length):
    count = key_blk.shape[0]
    raw = jnp.einsum(
        "qhd,khd->hqk",
        query_blk.reshape(-1, HEADS, HEAD_DIM),
        key_blk.reshape(count, HEADS, HEAD_DIM),
        preferred_element_type=jnp.float32,
    )
    position = owner * count + jnp.arange(count, dtype=jnp.int32)
    return jnp.where((position < length)[None, None, :], raw * HEAD_DIM ** (-0.5), masked_score)


def block_grads(query_blk, grad_blk, log_blk, delta_blk, key_blk, value_blk, owner, length):
    rows = query_blk.shape[0]
    count = key_blk.shape[0]
    scores = head_scores(query_blk, key_blk, owner, length)
    probs = jnp.exp(scores - log_blk[:, :, None])
    probs_low = probs.astype(jnp.bfloat16)
    grad_heads = grad_blk.reshape(rows, HEADS, HEAD_DIM)
    query_heads = query_blk.reshape(rows, HEADS, HEAD_DIM)
    key_heads = key_blk.reshape(count, HEADS, HEAD_DIM)
    value_heads = value_blk.reshape(count, HEADS, HEAD_DIM)
    prob_grad = jnp.einsum(
        "qhd,khd->hqk", grad_heads, value_heads, preferred_element_type=jnp.float32
    )
    score_grad = (probs * (prob_grad - delta_blk[:, :, None])).astype(jnp.bfloat16)
    value_term = jnp.einsum(
        "hqk,qhd->khd", probs_low, grad_heads, preferred_element_type=jnp.float32
    )
    key_term = jnp.einsum(
        "hqk,qhd->khd", score_grad, query_heads, preferred_element_type=jnp.float32
    ) * HEAD_DIM ** (-0.5)
    query_term = jnp.einsum(
        "hqk,khd->qhd", score_grad, key_heads, preferred_element_type=jnp.float32
    ) * HEAD_DIM ** (-0.5)
    return (
        query_term.reshape(rows, -1),
        key_term.reshape(count, -1),
        value_term.reshape(count, -1),
    )


def body(
    tokens,
    lengths,
    w_query,
    b_query,
    w_key,
    w_value,
    b_value,
    w_out,
    b_out,
    gain_one,
    shift_one,
    w_up,
    b_up,
    w_down,
    b_down,
    gain_two,
    shift_two,
    cotangent,
):
    cycle = lax.axis_size("ctx")
    place = lax.axis_index("ctx")
    length = lengths[0]
    rows = tokens.shape[0]
    width = tokens.shape[1]
    gathered = (
        lax.all_gather(w_query, ("batch", "ctx"), axis=0, tiled=True),
        lax.all_gather(w_key, ("batch", "ctx"), axis=0, tiled=True),
        lax.all_gather(w_value, ("batch", "ctx"), axis=0, tiled=True),
        lax.all_gather(w_out, ("batch", "ctx"), axis=0, tiled=True),
        lax.all_gather(w_up, ("batch", "ctx"), axis=0, tiled=True),
        lax.all_gather(w_down, ("batch", "ctx"), axis=0, tiled=True),
        lax.all_gather(b_query, ("batch", "ctx"), axis=0, tiled=True),
        lax.all_gather(b_value, ("batch", "ctx"), axis=0, tiled=True),
        lax.all_gather(b_out, ("batch", "ctx"), axis=0, tiled=True),
        lax.all_gather(gain_one, ("batch", "ctx"), axis=0, tiled=True),
        lax.all_gather(shift_one, ("batch", "ctx"), axis=0, tiled=True),
        lax.all_gather(b_up, ("batch", "ctx"), axis=0, tiled=True),
        lax.all_gather(b_down, ("batch", "ctx"), axis=0, tiled=True),
        lax.all_gather(gain_two, ("batch", "ctx"), axis=0, tiled=True),
        lax.all_gather(shift_two, ("batch", "ctx"), axis=0, tiled=True),
    )
    query_full, key_full, value_full, out_full, up_full, down_full = gathered[:6]
    small = [item.astype(jnp.float32) for item in gathered[6:]]
    (
        bias_query,
        bias_value,
        bias_out,
        gain_first,
        shift_first,
        bias_up,
        bias_down,
        gain_second,
        shift_second,
    ) = small
    query_low = (
        jnp.dot(tokens, query_full, preferred_element_type=jnp.float32) + bias_query
    ).astype(jnp.bfloat16)
    key_low = jnp.dot(tokens, key_full, preferred_element_type=jnp.float32).astype(jnp.bfloat16)
    value_low = (
        jnp.dot(tokens, value_full, preferred_element_type=jnp.float32) + bias_value
    ).astype(jnp.bfloat16)
    start_top = jnp.full((HEADS, rows), masked_score, jnp.float32)
    start_total = jnp.zeros((HEADS, rows), jnp.float32)
    start_sum = jnp.zeros((rows, HEADS, HEAD_DIM), jnp.float32)

    def running(state, pair, owner):
        top, total, summed = state
        scores = head_scores(query_low, pair[0], owner, length)
        new_top = jnp.maximum(top, jnp.max(scores, -1))
        factor = jnp.exp(top - new_top)
        expos = jnp.exp(scores - new_top[:, :, None])
        total = total * factor + jnp.sum(expos, -1)
        summed = summed * factor.T[:, :, None] + jnp.einsum(
            "hqk,khd->qhd",
            expos.astype(jnp.bfloat16),
            pair[1].reshape(-1, HEADS, HEAD_DIM),
            preferred_element_type=jnp.float32,
        )
        return (new_top, total, summed)

    def run_step(step, carry):
        pair, state = carry
        state = running(state, pair, (place - step) % cycle)
        pair = shifted((pair[0], pair[1]), "ctx", 1)
        return (pair, state)

    pair, state = lax.fori_loop(
        0, cycle - 1, run_step, ((key_low, value_low), (start_top, start_total, start_sum))
    )
    top, total, summed = running(state, pair, (place + 1) % cycle)
    log_total = top + jnp.log(total)
    attended = (summed / total.T[:, :, None]).reshape(rows, width)
    mixed = attended.astype(jnp.bfloat16)
    projected = jnp.dot(mixed, out_full, preferred_element_type=jnp.float32) + bias_out
    first, first_back = jax.vjp(
        normalize, tokens.astype(jnp.float32) + projected, gain_first, shift_first
    )
    first_low = first.astype(jnp.bfloat16)
    inner = jnp.dot(first_low, up_full, preferred_element_type=jnp.float32) + bias_up
    active, gelu_back = jax.vjp(gelu_exact, inner)
    active_low = active.astype(jnp.bfloat16)
    branch = jnp.dot(active_low, down_full, preferred_element_type=jnp.float32) + bias_down
    result, second_back = jax.vjp(normalize, first + branch, gain_second, shift_second)
    output = result.astype(jnp.bfloat16)
    query_back, key_back, value_back, out_back, up_back, down_back = (
        query_full,
        key_full,
        value_full,
        out_full,
        up_full,
        down_full,
    )
    grad_second, grad_gain_two, grad_shift_two = second_back(cotangent.astype(jnp.float32))
    branch_grad = grad_second.astype(jnp.bfloat16)
    grad_b_down = jnp.sum(branch_grad.astype(jnp.float32), 0)
    grad_w_down = jnp.einsum(
        "tf,td->fd", active_low, branch_grad, preferred_element_type=jnp.float32
    )
    active_grad = jnp.einsum(
        "td,fd->tf", branch_grad, down_back, preferred_element_type=jnp.float32
    )
    inner_grad = gelu_back(active_grad)[0].astype(jnp.bfloat16)
    grad_b_up = jnp.sum(inner_grad.astype(jnp.float32), 0)
    grad_w_up = jnp.einsum("td,tf->df", first_low, inner_grad, preferred_element_type=jnp.float32)
    first_grad = (
        jnp.einsum("tf,df->td", inner_grad, up_back, preferred_element_type=jnp.float32)
        + grad_second
    )
    grad_first, grad_gain_one, grad_shift_one = first_back(first_grad)
    proj_grad = grad_first.astype(jnp.bfloat16)
    grad_b_out = jnp.sum(proj_grad.astype(jnp.float32), 0)
    grad_w_out = jnp.einsum("td,te->de", mixed, proj_grad, preferred_element_type=jnp.float32)
    mixed_grad = jnp.einsum(
        "te,de->td", proj_grad, out_back, preferred_element_type=jnp.float32
    ).astype(jnp.bfloat16)
    delta = jnp.sum(
        (mixed_grad.astype(jnp.float32) * attended).reshape(rows, HEADS, HEAD_DIM), -1
    ).T
    zeros = jnp.zeros((rows, width), jnp.float32)

    def move_key_grads(grads):
        return (
            shifted(grads[0].astype(jnp.bfloat16), "ctx", 1).astype(jnp.float32),
            shifted(grads[1].astype(jnp.bfloat16), "ctx", 1).astype(jnp.float32),
        )

    def key_step(step, carry):
        blocks, grads, query_acc = carry
        query_term, key_term, value_term = block_grads(
            query_low,
            mixed_grad,
            log_total,
            delta,
            blocks[0],
            blocks[1],
            (place - step) % cycle,
            length,
        )
        grads = move_key_grads((grads[0] + key_term, grads[1] + value_term))
        blocks = shifted((blocks[0], blocks[1]), "ctx", 1)
        return (blocks, grads, query_acc + query_term)

    blocks, grads, query_acc = lax.fori_loop(
        0, cycle - 1, key_step, ((key_low, value_low), (zeros, zeros), zeros)
    )
    query_term, key_term, value_term = block_grads(
        query_low, mixed_grad, log_total, delta, blocks[0], blocks[1], (place + 1) % cycle, length
    )
    key_acc, value_acc = move_key_grads((grads[0] + key_term, grads[1] + value_term))
    query_acc = query_acc + query_term
    query_grad = query_acc.astype(jnp.bfloat16)
    key_grad = key_acc.astype(jnp.bfloat16)
    value_grad = value_acc.astype(jnp.bfloat16)
    grad_b_query = jnp.sum(query_grad.astype(jnp.float32), 0)
    grad_b_value = jnp.sum(value_grad.astype(jnp.float32), 0)
    grad_w_query = jnp.einsum("td,te->de", tokens, query_grad, preferred_element_type=jnp.float32)
    grad_w_key = jnp.einsum("td,te->de", tokens, key_grad, preferred_element_type=jnp.float32)
    grad_w_value = jnp.einsum("td,te->de", tokens, value_grad, preferred_element_type=jnp.float32)
    token_grad = grad_first + jnp.einsum(
        "te,de->td", query_grad, query_back, preferred_element_type=jnp.float32
    )
    token_grad = token_grad + jnp.einsum(
        "te,de->td", key_grad, key_back, preferred_element_type=jnp.float32
    )
    token_grad = token_grad + jnp.einsum(
        "te,de->td", value_grad, value_back, preferred_element_type=jnp.float32
    )
    grad_tokens = token_grad.astype(jnp.bfloat16)
    sharded = (
        lax.psum_scatter(grad_w_query, ("batch", "ctx"), scatter_dimension=0, tiled=True),
        lax.psum_scatter(grad_b_query, ("batch", "ctx"), scatter_dimension=0, tiled=True),
        lax.psum_scatter(grad_w_key, ("batch", "ctx"), scatter_dimension=0, tiled=True),
        lax.psum_scatter(grad_w_value, ("batch", "ctx"), scatter_dimension=0, tiled=True),
        lax.psum_scatter(grad_b_value, ("batch", "ctx"), scatter_dimension=0, tiled=True),
        lax.psum_scatter(grad_w_out, ("batch", "ctx"), scatter_dimension=0, tiled=True),
        lax.psum_scatter(grad_b_out, ("batch", "ctx"), scatter_dimension=0, tiled=True),
        lax.psum_scatter(grad_gain_one, ("batch", "ctx"), scatter_dimension=0, tiled=True),
        lax.psum_scatter(grad_shift_one, ("batch", "ctx"), scatter_dimension=0, tiled=True),
        lax.psum_scatter(grad_w_up, ("batch", "ctx"), scatter_dimension=0, tiled=True),
        lax.psum_scatter(grad_b_up, ("batch", "ctx"), scatter_dimension=0, tiled=True),
        lax.psum_scatter(grad_w_down, ("batch", "ctx"), scatter_dimension=0, tiled=True),
        lax.psum_scatter(grad_b_down, ("batch", "ctx"), scatter_dimension=0, tiled=True),
        lax.psum_scatter(grad_gain_two, ("batch", "ctx"), scatter_dimension=0, tiled=True),
        lax.psum_scatter(grad_shift_two, ("batch", "ctx"), scatter_dimension=0, tiled=True),
    )
    return (
        output,
        grad_tokens,
        sharded[0],
        sharded[1],
        sharded[2],
        sharded[3],
        sharded[4],
        sharded[5],
        sharded[6],
        sharded[7],
        sharded[8],
        sharded[9],
        sharded[10],
        sharded[11],
        sharded[12],
        sharded[13],
        sharded[14],
    )


def normal_parts(resid):
    center = resid - jnp.mean(resid, -1, keepdims=True)
    spread = jnp.mean(center * center, -1, keepdims=True)
    scale = lax.rsqrt(spread + epsilon)
    return center * scale, scale


def normal_back(hat, scale, grad):
    inner = jnp.mean(grad * hat, -1, keepdims=True)
    return scale * (grad - jnp.mean(grad, -1, keepdims=True) - hat * inner)


def dot(left, right, dims=((1,), (0,))):
    return lax.dot_general(left, right, (dims, ((), ())), preferred_element_type=jnp.float32)


def head_rows(block, head, extra):
    row = lax.broadcasted_iota(jnp.int32, block.shape, 0)
    keep = (row >= head * HEAD_DIM) & (row < (head + 1) * HEAD_DIM)
    if extra:
        keep = keep | (row >= extra)
    return jnp.where(keep, block, jnp.zeros_like(block))


def head_lanes(block, head):
    lane = lax.broadcasted_iota(jnp.int32, block.shape, 1)
    keep = (lane >= head * HEAD_DIM) & (lane < (head + 1) * HEAD_DIM)
    return jnp.where(keep, block, jnp.zeros_like(block))


def copied_kernel(kernel, first, far, count, shapes, *refs):
    operands, refs = refs[:count], refs[count:]
    results, refs = refs[: len(shapes)], refs[len(shapes) :]
    moved = [i for i in range(count) if i >= first and i not in far]
    taken, refs = refs[: len(moved)], refs[len(moved) :]
    given, refs = refs[: len(shapes)], refs[len(shapes) :]
    coming, going, rest = refs[0], refs[1], refs[2:]
    local = list(operands)
    copies = []
    for index, at in enumerate(moved):
        copies.append(pltpu.make_async_copy(operands[at], taken[index], coming.at[index]))
        local[at] = taken[index]
    for copy in copies:
        copy.start()
    for copy in copies:
        copy.wait()
    copies = [
        pltpu.make_async_copy(given[index], results[index], going.at[index])
        for index in range(len(shapes))
    ]
    kernel(*local, *given, *rest, leave=lambda *which: [copies[index].start() for index in which])
    for copy in copies:
        copy.wait()


def one_step(
    kernel, operands, shapes, flops, name, first=1, far=(), scratch=(), exps=0, limit=14
):
    specs = []
    for index in range(len(operands)):
        if index < first:
            specs.append(pl.BlockSpec(memory_space=pltpu.SMEM))
        elif index in far:
            specs.append(pl.BlockSpec(memory_space=pl.ANY))
        else:
            specs.append(pl.BlockSpec(memory_space=pltpu.HBM))
    moved = [
        pltpu.VMEM(operand.shape, operand.dtype)
        for index, operand in enumerate(operands)
        if index >= first and index not in far
    ]
    given = [pltpu.VMEM(*shape) for shape in shapes]
    return pl.pallas_call(
        functools.partial(copied_kernel, kernel, first, far, len(operands), shapes),
        in_specs=specs,
        out_specs=[pl.BlockSpec(memory_space=pltpu.HBM)] * len(shapes),
        out_shape=[pltpu.HBM(*shape) for shape in shapes],
        scratch_shapes=moved
        + given
        + [pltpu.SemaphoreType.DMA((len(moved),)), pltpu.SemaphoreType.DMA((len(shapes),))]
        + list(scratch),
        compiler_params=pltpu.CompilerParams(vmem_limit_bytes=limit * 2**20),
        cost_estimate=pl.CostEstimate(
            flops=flops,
            bytes_accessed=sum(operand.size * operand.dtype.itemsize for operand in operands),
            transcendentals=exps,
        ),
        name=name,
    )(*operands)


def turn(block):
    return jnp.transpose(block.astype(jnp.float32)).astype(block.dtype)


def attend_kernel(heads, chips, places, *refs, leave):
    own, others = refs[:chips], refs[chips : 2 * chips]
    weight, bias_query, bias_value = refs[2 * chips : 2 * chips + 3]
    refs = refs[2 * chips + 3 :]
    mine_ref, query, key, value, att, log = refs[:6]
    sent, (every, query_t, value_t, mixed) = refs[6 : 6 + chips], refs[6 + chips :]
    low, f32 = jnp.bfloat16, jnp.float32
    width = heads * HEAD_DIM
    count, rows, depth = every.shape
    spare = key.shape[1] - width

    for distance in range(chips):
        slot = lax.rem(places[0] - distance + chips, chips)
        every[slot] = own[distance][:rows, :]
        every[chips + slot] = others[distance][:rows, :]
    tokens = every[...].reshape(count * rows, depth)
    mine = chips * rows
    mine_ref[...] = tokens[:mine]
    first = dot(tokens[:mine], weight[:, :width]) + bias_query[...]
    first = (first.astype(low).astype(f32) * HEAD_DIM ** (-0.5)).astype(low)
    query[...] = first
    one = lax.broadcasted_iota(jnp.int32, (spare, mine), 0) == 0
    query_t[...] = jnp.concatenate([turn(first), jnp.where(one, 1.0, 0.0).astype(low)], 0)
    second = dot(tokens, weight[:, width : 2 * width]).astype(low)
    row = lax.broadcasted_iota(jnp.int32, (rows, spare), 0)
    lane = lax.broadcasted_iota(jnp.int32, (rows, spare), 1)
    for block in range(count):
        hide = jnp.where((row < places[1 + block]) | (lane > 0), 0.0, masked_score)
        at = slice(block * rows, (block + 1) * rows)
        key[at, :] = jnp.concatenate([second[at].astype(f32), hide], 1).astype(low)
    third = (dot(tokens, weight[:, 2 * width :]) + bias_value[...]).astype(low)
    value[...] = third
    value_t[...] = turn(third)
    leave(0, 1, 2, 3)

    pieces = 2 if chips % 2 == 0 else 1
    for step in range(chips // pieces):
        span = slice(step * pieces * rows, (step + 1) * pieces * rows)
        for head in range(heads):
            scores = dot(key[...], head_rows(query_t[:, span], head, width))
            top = jnp.max(scores, 0, keepdims=True)
            expos = jnp.exp(scores - top)
            total = jnp.sum(expos, 0, keepdims=True)
            at = slice(head * HEAD_DIM, (head + 1) * HEAD_DIM)
            summed = dot(value_t[at, :], expos.astype(low)) / total
            att[at, span] = summed
            for piece in range(pieces):
                mixed[step * pieces + piece, at, :] = summed[
                    :, piece * rows : (piece + 1) * rows
                ].astype(low)
            log[head : head + 1, span] = top + jnp.log(total)
    for distance in range(chips):
        sent[distance][...] = mixed[lax.rem(places[0] + distance, chips)]
    leave(*range(4, 6 + chips))


def attend(heads, places, own, others, weight, bias_query, bias_value):
    chips = len(own)
    rows, depth = own[0].shape
    count = 2 * chips
    mine, keys = chips * rows, count * rows
    width = heads * HEAD_DIM
    wide = -(-(width + 1) // 128) * 128
    low, f32 = jnp.bfloat16, jnp.float32
    return one_step(
        functools.partial(attend_kernel, heads, chips),
        [places, *own, *others, weight, bias_query, bias_value],
        [
            ((mine, depth), low),
            ((mine, width), low),
            ((keys, wide), low),
            ((keys, width), low),
            ((width, mine), f32),
            ((heads, mine), f32),
        ]
        + [((width, rows), low)] * chips,
        flops=4 * heads * mine * keys * 256 + 6 * keys * depth * width,
        name="attend",
        scratch=[
            pltpu.VMEM((count, rows, depth), low),
            pltpu.VMEM((wide, mine), low),
            pltpu.VMEM((width, keys), low),
            pltpu.VMEM((chips, width, rows), low),
        ],
        exps=heads * mine * keys,
    )


def attend_back_kernel(heads, chips, places, query, key, value, att, log, *refs, leave):
    come_refs, refs = refs[:chips], refs[chips + 1 :]
    query_grad, kept, away, key_sum, value_sum, grad_t, query_t, key_t = refs
    low = jnp.bfloat16
    width, rows = come_refs[0].shape
    mine = chips * rows
    for distance in range(chips):
        slot = lax.rem(places[0] - distance + chips, chips)
        grad_t[slot] = come_refs[distance][...]
    one = lax.broadcasted_iota(jnp.int32, (key.shape[1] - width, mine), 0) == 0
    query_t[...] = jnp.concatenate([turn(query[...]), jnp.where(one, 1.0, 0.0).astype(low)], 0)
    key_t[...] = turn(key[:, :width])
    pieces = 2 if chips % 2 == 0 else 1
    for step in range(chips // pieces):
        span = slice(step * pieces * rows, (step + 1) * pieces * rows)
        come = jnp.concatenate([grad_t[step * pieces + piece] for piece in range(pieces)], 1)
        come_rows = turn(come)
        turned = []
        for head in range(heads):
            at = slice(head * HEAD_DIM, (head + 1) * HEAD_DIM)
            scores = dot(key[...], head_rows(query_t[:, span], head, width))
            probs = jnp.exp(scores - log[head : head + 1, span])
            prob_grad = dot(value[...], head_rows(come, head, 0))
            delta = jnp.sum(come[at].astype(jnp.float32) * att[at, span], 0, keepdims=True)
            score_grad = (probs * (prob_grad - delta)).astype(low)
            turned.append(dot(key_t[at, :], score_grad))
            key_term = dot(score_grad, head_lanes(query[span, :], head))
            value_term = dot(probs.astype(low), head_lanes(come_rows, head))
            if step == 0 and head == 0:
                key_sum[...] = key_term
                value_sum[...] = value_term
            else:
                key_sum[...] += key_term
                value_sum[...] += value_term
        gathered = jnp.concatenate(turned, 0) * HEAD_DIM ** (-0.5)
        query_grad[span, :] = jnp.transpose(gathered).astype(low)
    kept[...] = jnp.concatenate([key_sum[:mine, :], value_sum[:mine, :]], 1)
    away[...] = jnp.concatenate([key_sum[mine:, :], value_sum[mine:, :]], 1).astype(low)
    leave(0, 1, 2)


def attend_back(heads, places, query, key, value, att, log, come, marker):
    chips = len(come)
    mine, width = query.shape
    keys, wide = key.shape
    low, f32 = jnp.bfloat16, jnp.float32
    return one_step(
        functools.partial(attend_back_kernel, heads, chips),
        [places, query, key, value, att, log, *come, marker],
        [((mine, width), low), ((mine, 2 * width), f32), ((keys - mine, 2 * width), low)],
        flops=10 * heads * mine * keys * 256,
        name="attend_back",
        far=(6 + chips,),
        scratch=[
            pltpu.VMEM((keys, width), f32),
            pltpu.VMEM((keys, width), f32),
            pltpu.VMEM((chips, width, mine // chips), low),
            pltpu.VMEM((wide, mine), low),
            pltpu.VMEM((width, keys), low),
        ],
        exps=heads * mine * keys,
    )


def finish_kernel(
    places, mine, weight, query_grad, kept, come, short, marker, *refs, leave
):
    low, f32 = jnp.bfloat16, jnp.float32
    token_part, own_terms, away_terms, terms = refs
    owners, _, part, width = terms.shape
    pair = (kept[...] + come[...].astype(f32)).astype(low)
    grads = jnp.concatenate([query_grad[...].astype(f32), pair.astype(f32)], 1)
    sums = jnp.sum(grads, 0, keepdims=True)
    grads = grads.astype(low)
    part_grad = dot(grads, weight[...], ((1,), (1,))).astype(low)
    token_part[...] = part_grad.reshape(token_part.shape)
    leave(0)
    terms[...] = dot(mine[...], grads, ((0,), (0,))).reshape(terms.shape)
    core = places[1]
    count = short.shape[2]
    row = lax.broadcasted_iota(jnp.int32, (count, width), 0)
    below = jnp.where(row == count - 1, sums, 0.0)
    for index, ref, which in ((1, away_terms, 1 - core), (0, own_terms, core)):
        for owner in range(owners):
            block = [terms[owner, which], short[owner, which] + below]
            ref[owner] = jnp.concatenate(block, 0).astype(ref.dtype)
        leave(1 + index)


def finish(chips, places, mine, weight, query_grad, kept, come, short, marker):
    count, depth = mine.shape
    width = weight.shape[1]
    owners = short.shape[0]
    part = depth // (2 * owners)
    held = part + short.shape[2]
    return one_step(
        finish_kernel,
        [places, mine, weight, query_grad, kept, come, short, marker],
        [
            ((chips, count // chips, depth), jnp.bfloat16),
            ((owners, held, width), jnp.float32),
            ((owners, held, width), jnp.bfloat16),
        ],
        flops=4 * count * depth * width,
        name="finish",
        far=(7,),
        scratch=[pltpu.VMEM((owners, 2, part, width), jnp.float32)],
    )


def bundle_kernel(places, own, come, w_up, *outs, leave):
    f32 = jnp.float32
    teams, part, width = w_up.shape
    owners, held, group = own.shape
    chips = owners // teams
    for distance, out in enumerate(outs):
        team = lax.rem(places[0] + distance, teams)
        for chip in range(chips):
            owner = team * chips + chip
            block = own[owner] + come[owner].astype(f32)
            block = jnp.pad(block, ((0, 0), (0, width - group)))
            out[chip * held : (chip + 1) * held] = block.astype(out.dtype)
        out[chips * held :] = w_up[team]
        leave(distance)


def bundle(places, own, come, w_up):
    teams, part, width = w_up.shape
    owners, held, _ = own.shape
    shape = (owners // teams * held + part, width)
    return one_step(
        bundle_kernel,
        [places, own, come, w_up],
        [(shape, jnp.bfloat16)] * teams,
        flops=0,
        limit=8,
        name="bundle",
    )


def unpack_kernel(part, group, found, *outs, leave):
    chips, count, _ = found.shape
    blocks = [found[chip].astype(jnp.float32) for chip in range(chips)]
    for index in range(3):
        columns = slice(index * group, (index + 1) * group)
        outs[index][...] = jnp.concatenate([block[:part, columns] for block in blocks], 1)
    total = blocks[0]
    for block in blocks[1:]:
        total = total + block
    outs[3][...] = total[count - part :]
    outs[4][...] = total[part : count - part]
    outs[5][...] = jnp.concatenate([b[count - part - 1 : count - part] for b in blocks], 0)
    leave(*range(6))


def unpack(part, group, found):
    chips, count, width = found.shape
    shapes = [((part, width), jnp.float32)] * 4
    shapes.append(((count - 2 * part, width), jnp.float32))
    shapes.append(((chips, width), jnp.float32))
    return one_step(
        functools.partial(unpack_kernel, part, group),
        [found],
        shapes,
        flops=found.size,
        limit=8,
        name="unpack",
        first=0,
    )


def wait_kernel(*refs):
    pass


def after(block, *others, pinned=False):
    anywhere = pl.BlockSpec(memory_space=pl.ANY)
    shape = jax.ShapeDtypeStruct(block.shape, block.dtype)
    if pinned:
        block = pltpu.with_memory_space_constraint(block, pltpu.HBM)
        shape = pltpu.HBM(block.shape, block.dtype)
    return pl.pallas_call(
        wait_kernel,
        in_specs=[anywhere] * (1 + len(others)),
        out_specs=anywhere,
        out_shape=shape,
        input_output_aliases={0: 0},
        compiler_params=pltpu.CompilerParams(vmem_limit_bytes=2**20),
        name="after",
    )(block, *others)


def lay_kernel(tokens, w_out, both):
    both[...] = jnp.concatenate([tokens[...], w_out[...]], 0)


def lay(tokens, w_out):
    shape = (tokens.shape[0] + w_out.shape[0], tokens.shape[1])
    return pl.pallas_call(
        lay_kernel,
        in_specs=[pl.BlockSpec(memory_space=pltpu.VMEM)] * 2,
        out_specs=pl.BlockSpec(memory_space=pltpu.VMEM),
        out_shape=jax.ShapeDtypeStruct(shape, tokens.dtype),
        name="lay",
    )(tokens, w_out)


def pack_kernel(chips, w_query, w_key, w_value, vectors, b_up, out):
    part = w_query.shape[0]
    group = w_query.shape[1] // chips
    count = vectors.shape[0]
    rest = out.shape[1] - part
    short = jnp.concatenate(
        [
            jnp.pad(vectors[...].astype(jnp.float32), ((0, rest - count), (0, 128 - part))),
            jnp.pad(
                b_up[...].astype(jnp.float32),
                ((0, rest - 1), (0, 3 * group - 128 - b_up.shape[1])),
            ),
        ],
        1,
    )
    for index in range(chips):
        columns = slice(index * group, (index + 1) * group)
        block = jnp.concatenate(
            [item[:, columns].astype(jnp.float32) for item in (w_query, w_key, w_value)], 1
        )
        both = jnp.concatenate([block, short], 0)
        spare = out.shape[2] - both.shape[1]
        out[index] = jnp.pad(both, ((0, 0), (0, spare))).astype(jnp.bfloat16)


def pack(chips, w_query, w_key, w_value, vectors, b_up, held):
    part, width = w_query.shape
    return pl.pallas_call(
        functools.partial(pack_kernel, chips),
        in_specs=[pl.BlockSpec(memory_space=pltpu.VMEM)] * 5,
        out_specs=pl.BlockSpec(memory_space=pltpu.VMEM),
        out_shape=jax.ShapeDtypeStruct((chips, held, width), jnp.bfloat16),
        name="pack",
    )(w_query, w_key, w_value, vectors, b_up)


def share_kernel(packed, w_up, out):
    teams, count, width = out.shape
    chips, held, _ = packed.shape
    for team in range(teams):
        for chip in range(chips):
            out[team, chip * held : (chip + 1) * held] = packed[chip]
        out[team, chips * held :] = w_up[:, team * width : (team + 1) * width]


def share(teams, packed, w_up):
    chips, held, width = packed.shape
    part, hidden = w_up.shape
    return pl.pallas_call(
        share_kernel,
        in_specs=[pl.BlockSpec(memory_space=pltpu.VMEM)] * 2,
        out_specs=pl.BlockSpec(memory_space=pltpu.VMEM),
        out_shape=jax.ShapeDtypeStruct(
            (teams, chips * held + part, hidden // teams), jnp.bfloat16
        ),
        name="share",
    )(packed, w_up)


def pick(blocks, index, axis=0):
    return lax.dynamic_index_in_dim(blocks, index, axis, keepdims=False)


def ordered(found, me):
    count = len(found)
    rising = [found[count - 1 - i] for i in range(count)]
    twice = jnp.stack(rising + rising[:-1], 0)
    return lax.dynamic_slice_in_dim(twice, count - 1 - me, count, 0)


def layer_split(
    tokens,
    lengths,
    w_query,
    b_query,
    w_key,
    w_value,
    b_value,
    w_out,
    b_out,
    gain_one,
    shift_one,
    w_up,
    b_up,
    w_down,
    b_down,
    gain_two,
    shift_two,
    cotangent,
):
    f32, low = jnp.float32, jnp.bfloat16
    teams = lax.axis_size("batch")
    chips = lax.axis_size("ctx") // 2
    team = lax.axis_index("batch")
    place = lax.axis_index("ctx")
    chip, core = place // 2, place % 2
    rows, width = tokens.shape
    part = w_query.shape[0]
    hidden = w_up.shape[1]
    quarter = hidden // teams
    heads = HEADS // chips
    group = heads * HEAD_DIM
    length = lengths[0]

    def to_chip(block, distance):
        route = [(i, (i // 2 + distance) % chips * 2 + i % 2) for i in range(2 * chips)]
        return lax.ppermute(block, "ctx", route)

    def to_core(block):
        return lax.ppermute(block, "ctx", [(i, i ^ 1) for i in range(2 * chips)])

    def to_team(block, distance):
        return lax.ppermute(block, "batch", [(i, (i + distance) % teams) for i in range(teams)])

    def from_chips(block):
        return [block] + [to_chip(block, d) for d in range(1, chips)]

    def from_teams(block):
        return [block] + [to_team(block, d) for d in range(1, teams)]

    def swap_chips(blocks, axis=0):
        return [pick(blocks, chip, axis)] + [
            to_chip(pick(blocks, (chip + d) % chips, axis), d) for d in range(1, chips)
        ]

    def swap_teams(blocks, axis=0):
        return [pick(blocks, team, axis)] + [
            to_team(pick(blocks, (team + d) % teams, axis), d) for d in range(1, teams)
        ]

    same_core = [[2 * z + c for z in range(chips)] for c in range(2)]

    def trade_chips(blocks):
        return lax.all_to_all(blocks, "ctx", 0, 0, axis_index_groups=same_core)

    def trade_teams(blocks):
        return lax.all_to_all(blocks, "batch", 0, 0)

    def both_cores(block, axis):
        other = to_core(block)
        first = jnp.where(core == 0, block, other)
        second = jnp.where(core == 0, other, block)
        return jnp.stack([first, second], axis)

    def cores_sum(terms, axis):
        away = to_core(pick(terms, 1 - core, axis).astype(low))
        return pick(terms, core, axis).astype(f32) + away.astype(f32)

    def total(blocks):
        result = blocks[0].astype(f32)
        for block in blocks[1:]:
            result = result + block.astype(f32)
        return result

    def return_teams(blocks):
        return total(
            [blocks[0]] + [to_team(blocks[d].astype(low), -d) for d in range(1, teams)]
        )

    vectors = (
        b_query,
        b_value,
        b_out,
        gain_one,
        shift_one,
        b_down,
        gain_two,
        shift_two,
    )
    held = -(-(part + len(vectors)) // 16) * 16
    laid = lay(tokens, w_out)
    packed = pack(
        chips,
        w_query,
        w_key,
        w_value,
        jnp.stack(vectors),
        b_up[None],
        held,
    )
    packed = trade_chips(packed)
    pieces = from_chips(after(laid, packed, pinned=True))
    traded = trade_teams(share(teams, packed, w_up))
    up_blocks = traded[:, chips * held :]
    packed = both_cores(traded[:, : chips * held].reshape(teams, chips, held, width), 2)
    w_heads = packed[:, :, :, :part, : 3 * group].reshape(width, 3 * group)
    shorts = packed[:, :, :, part:].reshape(teams * chips * 2, held - part, width)

    rows_of = shorts[:, :, :part].transpose(1, 0, 2).reshape(held - part, width)
    bias_query, bias_value, bias_out, gain_first, shift_first = rows_of[:5].astype(f32)
    bias_down, gain_second, shift_second = rows_of[5:8].astype(f32)
    bias_up = shorts[:, 0, 128 : 128 + b_up.shape[0]].reshape(-1).astype(f32)
    bias_up = lax.dynamic_slice_in_dim(bias_up, team * quarter, quarter)
    bias_query = lax.dynamic_slice_in_dim(bias_query, chip * group, group)
    bias_value = lax.dynamic_slice_in_dim(bias_value, chip * group, group)

    others = [to_core(tokens)] + [to_core(piece) for piece in pieces[1:]]
    starts = jnp.arange(chips, dtype=jnp.int32) * (2 * rows)
    starts = jnp.concatenate([starts + core * rows, starts + (1 - core) * rows])
    places = jnp.concatenate([chip[None], length - starts])

    out_rel = [w_out] + [piece[rows:] for piece in pieces[1:]]
    later = jnp.concatenate([up_blocks.reshape(teams * part, quarter), w_down], 0)
    later = lax.all_gather(later, "ctx", axis=0)
    out_blocks = after(ordered(out_rel, chip), w_heads)
    out_blocks = trade_teams(jnp.broadcast_to(out_blocks[None], (teams,) + out_blocks.shape))

    mine, query, key, value, attended, log_total, *mixed_out = attend(
        heads,
        places,
        [tokens] + pieces[1:],
        others,
        w_heads,
        bias_query[None],
        bias_value[None],
    )
    up_part = later[:, : teams * part].reshape(2 * chips, teams, part, quarter)
    up_part = up_part.transpose(1, 0, 2, 3).reshape(width, quarter)
    down_part = later[:, teams * part :].reshape(quarter, width)
    out_full = both_cores(after(out_blocks, log_total), 2).reshape(width, width)

    tn = ((0,), (0,))
    mixed_rel = [mixed_out[0]] + [to_chip(mixed_out[d], d) for d in range(1, chips)]
    mixed_t = ordered(mixed_rel, chip).reshape(width, rows)
    projected = dot(mixed_t, out_full, tn) + bias_out
    hat_one, scale_one = normal_parts(tokens.astype(f32) + projected)
    first = hat_one * gain_first + shift_first
    first_low = first.astype(low)

    wide = jnp.concatenate(from_teams(first_low), 0)
    inner = dot(wide, up_part) + bias_up
    cdf = 0.5 * (1.0 + lax.erf(inner * 2.0**-0.5))
    slope = cdf + inner * (jnp.exp(-0.5 * inner * inner) * (2.0 * math.pi) ** -0.5)
    active_low = (inner * cdf).astype(low)
    active_low, slope = lax.optimization_barrier((active_low, slope))
    branch_part = dot(active_low, down_part)
    branch = return_teams(branch_part.reshape(teams, rows, width)) + bias_down
    hat_two, scale_two = normal_parts(first + branch)
    output = (hat_two * gain_second + shift_second).astype(low)
    grad_out = cotangent.astype(f32)
    grad_gain_two = jnp.sum(grad_out * hat_two, 0)
    grad_shift_two = jnp.sum(grad_out, 0)
    grad_second = normal_back(hat_two, scale_two, grad_out * gain_second)
    branch_grad = grad_second.astype(low)
    grad_b_down = jnp.sum(branch_grad.astype(f32), 0)
    wide_grad = jnp.concatenate(from_teams(branch_grad), 0)
    active_grad = dot(wide_grad, down_part, ((1,), (1,)))
    inner_grad = (active_grad * slope).astype(low)
    first_part = dot(inner_grad, up_part, ((1,), (1,))).astype(low)
    first_part = first_part.reshape(teams, rows, width)
    leaving = [first_part[d] for d in range(teams)]
    come_back = [to_team(leaving[d], -d) for d in range(1, teams)]
    first_grad = total([leaving[0]] + come_back) + grad_second
    grad_b_up = jnp.sum(inner_grad.astype(f32), 0)
    grad_down = dot(active_low, after(wide_grad, leaving[1]), tn)
    grad_up = dot(wide, after(inner_grad, leaving[1]), tn)

    grad_gain_one = jnp.sum(first_grad * hat_one, 0)
    grad_shift_one = jnp.sum(first_grad, 0)
    grad_first = normal_back(hat_one, scale_one, first_grad * gain_first)
    proj_grad = grad_first.astype(low)
    grad_b_out = jnp.sum(proj_grad.astype(f32), 0)
    mixed_grad_t = dot(out_full, proj_grad, ((1,), (1,))).astype(low)
    mixed_grad_t = mixed_grad_t.reshape(chips, group, rows)
    leaving = [pick(mixed_grad_t, (chip + d) % chips) for d in range(chips)]
    grad_out_w = dot(mixed_t, after(proj_grad, leaving[1])).astype(low)
    out_sum = cores_sum(grad_out_w.reshape(teams, chips, 2, part, width), 2).astype(low)

    come = [leaving[0]] + [to_chip(leaving[d], d) for d in range(1, chips)]
    query_grad, kept, away = attend_back(
        heads, places, query, key, value, attended, log_total, come, out_sum
    )
    up_terms = grad_up.astype(low).reshape(teams, 2 * chips, part, quarter)
    up_terms = up_terms.transpose(1, 0, 2, 3).reshape(2 * chips, teams * part, quarter)
    down_terms = grad_down.astype(low).reshape(2 * chips, -1, width)
    sums = lax.psum_scatter(
        jnp.concatenate([up_terms, down_terms], 1), "ctx", scatter_dimension=0, tiled=False
    )
    up_sum = sums[: teams * part].reshape(teams, part, quarter)

    out_traded = trade_teams(out_sum)
    small = (
        grad_b_out,
        grad_gain_one,
        grad_shift_one,
        grad_b_down,
        grad_gain_two,
        grad_shift_two,
    )
    small = jnp.stack([item.reshape(teams * chips, 2, part) for item in small], 2)
    small = jnp.pad(small, ((0, 0),) * 2 + ((0, held - part - len(vectors) + 2), (0, 128 - part)))
    tall = lax.dynamic_update_slice_in_dim(
        jnp.zeros((hidden,), f32), grad_b_up, team * quarter, 0
    ).reshape(teams * chips, 2, 1, -1)
    lanes = 3 * group - 128 - tall.shape[-1]
    tall = jnp.pad(tall, ((0, 0),) * 2 + ((0, held - part - 1), (0, lanes)))
    token_part, own_terms, away_terms = finish(
        chips,
        jnp.stack([chip, core]),
        mine,
        w_heads,
        query_grad,
        kept,
        to_core(away),
        jnp.concatenate([small, tall], 3),
        out_traded,
    )
    bundles = bundle(team[None], own_terms, to_core(away_terms), up_sum)
    traded = [bundles[0]] + [to_team(bundles[d], d) for d in range(1, teams)]
    token_come = trade_chips(token_part)
    token_come = after(token_come, *traded[1:])
    token_grad = grad_first + jnp.sum(token_come.astype(f32), 0)
    grad_tokens = token_grad.astype(low)
    out_up = ordered([block[-part:] for block in traded], team)
    out_up = out_up.transpose(1, 0, 2).reshape(part, hidden).astype(f32)
    terms = total([block[:-part] for block in traded]).astype(low)
    out_down = after(sums, traded[1])[teams * part :].astype(f32)
    out_sum = jnp.sum(out_traded.astype(f32), 0).astype(low)
    terms = jnp.concatenate([terms.reshape(chips, held, width), out_sum], 1)
    found = trade_chips(after(terms, grad_tokens))
    out_query, out_key, out_value, out_out, short_sum, sums = unpack(part, group, found)
    vec = [short_sum[i, :part] for i in range(6)]
    out_b_up = short_sum[0, 128 : 128 + b_up.shape[0]]
    own_sums = lax.dynamic_slice(sums, (team, 0), (1, 3 * group))[0].reshape(3, group)
    own_sums = lax.dynamic_slice(own_sums, (0, place * part), (3, part))
    return (
        output,
        grad_tokens,
        out_query,
        own_sums[0],
        out_key,
        out_value,
        own_sums[2],
        out_out,
        vec[0],
        vec[1],
        vec[2],
        out_up,
        out_b_up,
        out_down,
        vec[3],
        vec[4],
        vec[5],
    )


def solution(mesh):
    in_specs = (
        P(("batch", "ctx"), None),
        P("batch"),
        P(("batch", "ctx"), None),
        P(("batch", "ctx")),
        P(("batch", "ctx"), None),
        P(("batch", "ctx"), None),
        P(("batch", "ctx")),
        P(("batch", "ctx"), None),
        P(("batch", "ctx")),
        P(("batch", "ctx")),
        P(("batch", "ctx")),
        P(("batch", "ctx"), None),
        P(("batch", "ctx")),
        P(("batch", "ctx"), None),
        P(("batch", "ctx")),
        P(("batch", "ctx")),
        P(("batch", "ctx")),
        P(("batch", "ctx"), None),
    )
    out_specs = (
        P(("batch", "ctx"), None),
        P(("batch", "ctx"), None),
        P(("batch", "ctx"), None),
        P(("batch", "ctx")),
        P(("batch", "ctx"), None),
        P(("batch", "ctx"), None),
        P(("batch", "ctx")),
        P(("batch", "ctx"), None),
        P(("batch", "ctx")),
        P(("batch", "ctx")),
        P(("batch", "ctx")),
        P(("batch", "ctx"), None),
        P(("batch", "ctx")),
        P(("batch", "ctx"), None),
        P(("batch", "ctx")),
        P(("batch", "ctx")),
        P(("batch", "ctx")),
    )
    places = mesh.shape["ctx"]
    whole_heads = places % 2 == 0 and HEADS % (places // 2) == 0
    step = layer_split if whole_heads else body
    return jax.shard_map(step, mesh=mesh, in_specs=in_specs, out_specs=out_specs, check_vma=False)
```
